128 devices in a mesh: pb: 4 (over x), pa: 32 (over z, y, core).
Axes of the slice: x: 4, y: 4, z: 4, core: 2. Of those that a mesh axis runs over, the one named last changes fastest.
Arguments:
- queries: bfloat16 [512, 32, 128], P('pb'), may hold values from -30 to 30
- passages: bfloat16 [256, 180, 128], P('pa'), may hold values from -1.8 to 1.8
- pair_mask: int32 [64, 32], P('pb', 'pa'), may hold values from 0 to 1, as said below
- positive: int32 [512], P('pb'), may hold values from 0 to 255, as said below
Outputs:
- loss: float32 [512], P(('pb', 'pa'))
- grad_queries: float32 [512, 32, 128], P(('pb', 'pa'))
- grad_passages: float32 [256, 180, 128], P('pa')
The draws below stay inside these ranges and needn't reach their ends.
Inputs may be any that keep to these rules, and one draw needn't show every extreme that they name: `pair_mask`: every query block is paired with the block of each of its queries' positives. The positive of a query lies in a passage block paired with the query's block.
All inputs are finite; a program needn't handle non-finite values.
Results may differ from the reference program's by a relative error of at most 0.0029.
Values may be sent and summed in bfloat16 or wider, within the bound.
No kernel may reach another device: no remote copies, remote signals or barrier semaphores. Data moves between devices by JAX's collectives and lax.ppermute only.
A program may use at most 128 MiB of HBM per device.

```python
import jax
import jax.numpy as jnp
from jax import lax

D = 128
LQ = 32
LP = 180
B = 8
NQB = 64
NPB = 32
NQ = 512
NP = 256


def pairing(key):
    shift_key = jax.random.fold_in(key, 101)
    item_key = jax.random.fold_in(key, 102)
    heat_key = jax.random.fold_in(key, 103)
    roll_key = jax.random.fold_in(key, 104)
    query_block = jnp.arange(NQ, dtype=jnp.int32) // B
    shifts = jax.random.randint(shift_key, (NQ,), 0, 2, dtype=jnp.int32)
    items_drawn = jax.random.randint(item_key, (NQ,), 0, B, dtype=jnp.int32)
    positive = (query_block * 7 + shifts) % NPB * B + items_drawn
    heat = jax.random.randint(heat_key, (NPB,), 0, 4, dtype=jnp.int32)
    cutoffs = jnp.array([2, 10, 30, 90], dtype=jnp.int32)[heat]
    rolls = jax.random.randint(roll_key, (NQB, NPB), 0, 100, dtype=jnp.int32)
    mask = (rolls < cutoffs[None, :]).astype(jnp.int32)
    rows_idx = jnp.arange(NQB, dtype=jnp.int32)[:, None]
    near = (rows_idx * 7 + jnp.arange(2, dtype=jnp.int32)[None, :]) % NPB
    mask = mask.at[jnp.broadcast_to(rows_idx, near.shape), near].set(1)
    return (positive, mask)


def passage_table(key):
    base = jax.random.normal(jax.random.fold_in(key, 500), (NP, LP, D), jnp.float32) * 0.3
    return jnp.clip(base, -1.8, 1.8)


def draw_positive(key, part):
    return pairing(key)[0]


def draw_pair_mask(key, part):
    return pairing(key)[1]


def draw_passages(key, part):
    return passage_table(key).astype(jnp.bfloat16)


def draw_queries(key, part):
    key = jax.random.fold_in(key, 7)
    base = jnp.clip(jax.random.normal(key, (NQ, LQ, D), jnp.float32) * 0.3, -1.8, 1.8)
    return base.astype(jnp.bfloat16)


def setup_inputs(seed: int = 0) -> dict:
    key_list = jax.random.split(jax.random.key(seed), 5)
    queries = draw_queries(jax.random.fold_in(key_list[4], 71), 0)
    passages = draw_passages(jax.random.fold_in(key_list[4], 71), 0)
    pair_mask = draw_pair_mask(jax.random.fold_in(key_list[4], 71), 0)
    positive = draw_positive(jax.random.fold_in(key_list[4], 71), 0)
    return {"queries": queries, "passages": passages, "pair_mask": pair_mask, "positive": positive}


very_low = -1.0e30
contrast_temp = 0.05


def block_sim(query_block, passage_block):
    return lax.dot_general(query_block, passage_block, (((1,), (1,)), ((), ())), preferred_element_type=jnp.float32)


def token_stats(similar):
    shaped = similar.reshape(B, LQ, B, LP)
    row_top = jnp.max(shaped, axis=3, keepdims=True)
    scaled = jnp.exp(shaped - row_top)
    tok_total = jnp.sum(scaled, axis=3, keepdims=True)
    return row_top, scaled, tok_total


def reference(queries, passages, pair_mask, positive):
    query_all = queries.reshape(NQB, B * LQ, D)
    passage_all = passages.reshape(NPB, B * LP, D)

    def score_of(qblock, pblock):
        row_top, scaled, tok_total = token_stats(block_sim(query_all[qblock], passage_all[pblock]))
        return jnp.mean(row_top[..., 0] + jnp.log(tok_total[..., 0]), axis=1)

    def forward(pair_index, scores):
        qblock = (pair_index // NPB).astype(jnp.int32)
        pblock = (pair_index % NPB).astype(jnp.int32)
        value = lax.cond(pair_mask[qblock, pblock] > 0, lambda: score_of(qblock, pblock),
                         lambda: jnp.full((B, B), very_low, jnp.float32))
        return lax.dynamic_update_slice(scores, value.reshape(1, B, 1, B), (qblock, jnp.int32(0), pblock, jnp.int32(0)))

    scores = jnp.full((NQB, B, NPB, B), very_low, jnp.float32)
    scores = lax.fori_loop(0, NQB * NPB, forward, scores).reshape(NQ, NP)
    active = scores > very_low / 2
    logits = jnp.where(active, scores / contrast_temp, very_low)
    row_max = jnp.max(logits, axis=1)
    total = jnp.sum(jnp.where(active, jnp.exp(logits - row_max[:, None]), 0.0), axis=1)
    pos_logit = jnp.take_along_axis(logits, positive.astype(jnp.int32)[:, None], axis=1)[:, 0]
    loss = row_max + jnp.log(total) - pos_logit
    onehot = (jnp.arange(NP, dtype=jnp.int32)[None, :] == positive.astype(jnp.int32)[:, None]).astype(jnp.float32)
    coef = (jnp.where(active, jnp.exp(logits - row_max[:, None]) / total[:, None], 0.0) - onehot) / (contrast_temp * LQ)
    coef = coef.reshape(NQB, B, NPB, B)

    def backward(pair_index, carry):
        qblock = (pair_index // NPB).astype(jnp.int32)
        pblock = (pair_index % NPB).astype(jnp.int32)

        def update(inner):
            grad_q, grad_p = inner
            query_block = query_all[qblock]
            passage_block = passage_all[pblock]
            row_top, scaled, tok_total = token_stats(block_sim(query_block, passage_block))
            weight = coef[qblock, :, pblock, :][:, None, :, None] * (scaled / tok_total)
            dsim = weight.astype(jnp.bfloat16).reshape(B * LQ, B * LP)
            grad_q = grad_q.at[qblock].add(jnp.dot(dsim, passage_block, preferred_element_type=jnp.float32))
            grad_p = grad_p.at[pblock].add(lax.dot_general(dsim, query_block, (((0,), (0,)), ((), ())), preferred_element_type=jnp.float32))
            return grad_q, grad_p

        return lax.cond(pair_mask[qblock, pblock] > 0, update, lambda inner: inner, carry)

    grad_q = jnp.zeros((NQB, B * LQ, D), jnp.float32)
    grad_p = jnp.zeros((NPB, B * LP, D), jnp.float32)
    grad_q, grad_p = lax.fori_loop(0, NQB * NPB, backward, (grad_q, grad_p))
    return loss, grad_q.reshape(NQ, LQ, D), grad_p.reshape(NP, LP, D)
```

```python
import jax
import jax.numpy as jnp
from jax import lax
from jax.experimental import pallas as pl
from jax.experimental.pallas import tpu as pltpu
from jax.sharding import PartitionSpec as P

very_low = -1e30
contrast_temp = 0.05
f32, bf16 = jnp.float32, jnp.bfloat16
VMEM = pl.BlockSpec(memory_space=pltpu.VMEM)
SMEM = pl.BlockSpec(memory_space=pltpu.SMEM)
B, LQ, LP, D = 8, 32, 180, 128
LPP = 192
MAIN = 176
QT = B * LQ


def iota(shape, dim):
    return lax.broadcasted_iota(jnp.int32, shape, dim)


def exact_dot(a, b):
    return jnp.dot(a, b, precision=lax.Precision.HIGHEST, preferred_element_type=f32)


def expand(row, blocks):
    count = blocks * B
    own = iota((blocks, count), 1) // B == iota((blocks, count), 0)
    pick = (iota((count, QT), 0) % B == iota((count, QT), 1) // LQ).astype(f32)
    return exact_dot(jnp.where(own, row, 0.0), pick)


def squeeze(wide, blocks):
    count = blocks * B
    pick = (iota((QT, count), 0) == LQ * (iota((QT, count), 1) % B)).astype(f32)
    own = iota((blocks, count), 1) // B == iota((blocks, count), 0)
    return jnp.sum(jnp.where(own, exact_dot(wide, pick), 0.0), axis=0, keepdims=True)


def pad_passages(p_ref, pad_ref):
    for p in range(B):
        padded = jnp.concatenate([p_ref[p].astype(f32), jnp.zeros((LPP - LP, D), f32)], axis=0)
        pad_ref[p] = padded.astype(bf16)


def passage_sim(pad_ref, p, qk):
    sim = lax.dot_general(pad_ref[p], qk, (((1,), (1,)), ((), ())), preferred_element_type=f32)
    tail = jnp.where(iota((LPP - MAIN, QT), 0) < LP - MAIN, sim[MAIN:], very_low)
    return sim[:MAIN], tail


def is_positive(pos_ref, active, blocks):
    pos = expand(pos_ref[...].astype(f32), blocks).astype(jnp.int32)
    item = iota((blocks, B, QT), 1) + lax.axis_index("pa") * B
    return (pos[:, None, :] == item) & active


def scores_kernel(mask_s, mask_v, pos_ref, q_ref, p_ref, send_ref, logit_ref, top_ref, tot_ref, pad_ref):
    blocks = mask_s.shape[0]
    pad_passages(p_ref, pad_ref)
    top_ref[...] = jnp.zeros_like(top_ref)
    tot_ref[...] = jnp.ones_like(tot_ref)

    @pl.loop(0, blocks)
    def _(k):
        @pl.when(mask_s[k, 0] > 0)
        def _():
            qk = q_ref[pl.ds(pl.multiple_of(k * QT, QT), QT), :]
            for p in range(B):
                main, tail = passage_sim(pad_ref, p, qk)
                top = jnp.maximum(
                    jnp.max(main, axis=0, keepdims=True), jnp.max(tail, axis=0, keepdims=True)
                )
                top_ref[k, p : p + 1] = top
                tot_ref[k, p : p + 1] = jnp.sum(
                    jnp.exp(main - top), axis=0, keepdims=True
                ) + jnp.sum(jnp.exp(tail - top), axis=0, keepdims=True)

    active = mask_v[...].reshape(blocks, 1, 1) > 0
    token_lse = (top_ref[...] + jnp.log(tot_ref[...])).reshape(blocks * B, QT)
    same = (iota((QT, QT), 0) // LQ == iota((QT, QT), 1) // LQ).astype(f32)
    score = (exact_dot(token_lse, same) / LQ).reshape(blocks, B, QT)
    logit = jnp.where(active, score / contrast_temp, very_low)
    logit_ref[...] = logit
    local_top = jnp.max(logit, axis=1, keepdims=True)
    local_total = jnp.sum(jnp.where(active, jnp.exp(logit - local_top), 0.0), axis=1)
    local_pos = jnp.sum(jnp.where(is_positive(pos_ref, active, blocks), logit, 0.0), axis=1)
    rows = [squeeze(x, blocks) for x in (local_top[:, 0, :], local_total, local_pos)]
    rows.append(jnp.zeros((5, blocks * B), f32))
    send_ref[...] = jnp.broadcast_to(jnp.concatenate(rows, axis=0)[None], send_ref.shape)


def grads_kernel(
    mask_s, mask_v, pos_ref, q_ref, p_ref, stat_ref, logit_ref, top_ref, tot_ref,
    loss_ref, gq_ref, own_ref, send1_ref, send2_ref, send3_ref,
    pad_ref, turn_ref, weight_ref, gp_ref,
):
    blocks = mask_s.shape[0]
    pad_passages(p_ref, pad_ref)
    for p in range(B):
        turn_ref[p] = pad_ref[p].astype(f32).T.astype(bf16)
    tops = stat_ref[:, 0, :]
    glob_top = jnp.max(tops, axis=0, keepdims=True)
    glob_total = jnp.sum(stat_ref[:, 1, :] * jnp.exp(tops - glob_top), axis=0, keepdims=True)
    glob_pos = jnp.sum(stat_ref[:, 2, :], axis=0, keepdims=True)
    loss_ref[...] = glob_top + jnp.log(glob_total) - glob_pos
    active = mask_v[...].reshape(blocks, 1, 1) > 0
    wide_top = expand(glob_top, blocks)[:, None, :]
    wide_total = expand(glob_total, blocks)[:, None, :]
    prob = jnp.where(active, jnp.exp(logit_ref[...] - wide_top) / wide_total, 0.0)
    onehot = is_positive(pos_ref, active, blocks).astype(f32)
    weight_ref[...] = (prob - onehot) / (contrast_temp * LQ) / tot_ref[...]
    gp_ref[...] = jnp.zeros_like(gp_ref)

    @pl.loop(0, blocks)
    def _(k):
        @pl.when(mask_s[k, 0] > 0)
        def _():
            qk = q_ref[pl.ds(pl.multiple_of(k * QT, QT), QT), :]
            turned = jnp.zeros((D, QT), f32)
            for p in range(B):
                main, tail = passage_sim(pad_ref, p, qk)
                top = top_ref[k, p : p + 1]
                weight = weight_ref[k, p : p + 1]
                dsim = jnp.concatenate(
                    [
                        (jnp.exp(main - top) * weight).astype(bf16),
                        (jnp.exp(tail - top) * weight).astype(bf16),
                    ],
                    axis=0,
                )
                gp_ref[p] += jnp.dot(dsim, qk, preferred_element_type=f32)
                turned += jnp.dot(turn_ref[p], dsim, preferred_element_type=f32)
            part = turned.T.astype(bf16)
            gq_ref[2 * k] = part[: QT // 2]
            gq_ref[2 * k + 1] = part[QT // 2 :]

        @pl.when(mask_s[k, 0] <= 0)
        def _():
            gq_ref[2 * k] = jnp.zeros((QT // 2, D), bf16)
            gq_ref[2 * k + 1] = jnp.zeros((QT // 2, D), bf16)

    mine = lax.axis_index("pb")
    for t in range(2):
        own_ref[t] = gp_ref[2 * mine + t]
        for s, send in ((1, send1_ref), (2, send2_ref), (3, send3_ref)):
            send[t] = gp_ref[2 * lax.rem(mine + s, 4) + t].astype(bf16)


def sum_kernel(own_ref, a_ref, b_ref, c_ref, out_ref):
    total = own_ref[...] + a_ref[...].astype(f32) + b_ref[...].astype(f32) + c_ref[...].astype(f32)
    out_ref[...] = total.astype(bf16)


def place_kernel(own_ref, a_ref, b_ref, c_ref, out_ref):
    mine = lax.axis_index("pb")
    for s, ref in ((0, own_ref), (1, a_ref), (2, b_ref), (3, c_ref)):
        owner = lax.rem(mine + 4 - s, 4)
        for t in range(2):
            out_ref[2 * owner + t] = ref[t].astype(f32)[:LP]


def rows_kernel(in_ref, out_ref):
    total = in_ref[0].astype(f32)
    for i in range(1, in_ref.shape[0]):
        total += in_ref[i].astype(f32)
    out_ref[...] = total


def call(kernel, out, n_in, smem_first=False, scratch=(), vmem=48 << 20):
    return pl.pallas_call(
        kernel,
        out_shape=out,
        in_specs=[SMEM if smem_first and i == 0 else VMEM for i in range(n_in)],
        out_specs=jax.tree.map(lambda _: VMEM, out),
        scratch_shapes=list(scratch),
        compiler_params=pltpu.CompilerParams(vmem_limit_bytes=vmem),
    )


def turn(x, s):
    return lax.ppermute(x, "pb", [(i, (i + s) % 4) for i in range(4)])


def on_device(queries, passages, pair_mask, positive):
    rows = queries.shape[0]
    blocks = rows // B
    peers = lax.axis_size("pa")
    shape = jax.ShapeDtypeStruct
    flat = queries.reshape(rows * LQ, D)
    pos = positive.reshape(1, rows)
    wide = shape((blocks, B, QT), f32)
    pad = pltpu.VMEM((B, LPP, D), bf16)
    send, logit, top, tot = call(
        scores_kernel, (shape((peers, 8, rows), f32), wide, wide, wide), 5, True, [pad]
    )(pair_mask, pair_mask, pos, flat, passages)
    stats = lax.all_to_all(send, "pa", 0, 0, tiled=True)
    piece = shape((2, LPP, D), bf16)
    loss, gq, own, send1, send2, send3 = call(
        grads_kernel,
        (shape((1, rows), f32), shape((peers, 4 * LQ, D), bf16), shape((2, LPP, D), f32), piece, piece, piece),
        9,
        True,
        [pad, pltpu.VMEM((B, D, LPP), bf16), pltpu.VMEM((blocks, B, QT), f32), pltpu.VMEM((B, LPP, D), f32)],
    )(pair_mask, pair_mask, pos, flat, passages, stats, logit, top, tot)
    got = [turn(x, s) for x, s in ((send1, 1), (send2, 2), (send3, 3))]
    gq_terms = lax.all_to_all(gq, "pa", 0, 0, tiled=True)
    mine = call(sum_kernel, piece, 4)(own, *got)
    others = [turn(mine, s) for s in (1, 2, 3)]
    grad_p = call(place_kernel, shape((B, LP, D), f32), 4)(mine, *others)
    grad_q = call(rows_kernel, shape((4 * LQ, D), f32), 1)(gq_terms).reshape(4, LQ, D)
    loss_rows = lax.dynamic_slice_in_dim(loss[0], lax.axis_index("pa") * 4, 4, 0)
    return loss_rows, grad_q, grad_p


def solution(mesh):
    placed = (P("pb", None, None), P("pa", None, None), P("pb", "pa"), P("pb"))
    return jax.shard_map(
        on_device,
        mesh=mesh,
        in_specs=placed,
        out_specs=(P(("pb", "pa")), P(("pb", "pa"), None, None), P("pa", None, None)),
        check_vma=False,
    )
```

```python
import jax
import jax.numpy as jnp
from jax import lax
from jax.experimental import pallas as pl
from jax.experimental.pallas import tpu as pltpu
from jax.sharding import PartitionSpec as P

very_low = -1e30
contrast_temp = 0.05
f32, bf16 = jnp.float32, jnp.bfloat16
VMEM = pl.BlockSpec(memory_space=pltpu.VMEM)
SMEM = pl.BlockSpec(memory_space=pltpu.SMEM)
B, LQ, LP, D = 8, 32, 180, 128
QT = B * LQ
PT = B * LP
turned_dims = (((1,), (1,)), ((), ()))


def iota(shape, dim):
    return lax.broadcasted_iota(jnp.int32, shape, dim)


def exact_dot(a, b):
    return jnp.dot(a, b, precision=lax.Precision.HIGHEST, preferred_element_type=f32)


def expand(row, blocks):
    count = blocks * B
    own = iota((blocks, count), 1) // B == iota((blocks, count), 0)
    pick = (iota((count, QT), 0) % B == iota((count, QT), 1) // LQ).astype(f32)
    return exact_dot(jnp.where(own, row, 0.0), pick)


def squeeze(wide, blocks):
    count = blocks * B
    pick = (iota((QT, count), 0) == LQ * (iota((QT, count), 1) % B)).astype(f32)
    own = iota((blocks, count), 1) // B == iota((blocks, count), 0)
    return jnp.sum(jnp.where(own, exact_dot(wide, pick), 0.0), axis=0, keepdims=True)


def list_tasks(mask_s, order):
    blocks = mask_s.shape[0]
    count = jnp.int32(0)
    for wanted in (True, False):
        for k in range(blocks):
            here = (mask_s[k] > 0) == wanted

            @pl.when(here)
            def _(k=k, count=count):
                order[count] = k

            count = count + here.astype(jnp.int32)
        if wanted:
            active = count
    return active


def active_blocks(mask_s):
    blocks = mask_s.shape[0]
    return jnp.stack([jnp.full((B, QT), mask_s[k], jnp.int32) for k in range(blocks)]) > 0


def pair_queries(q_ref, first, second):
    return jnp.concatenate(
        [q_ref[pl.ds(pl.multiple_of(k * QT, QT), QT), :] for k in (first, second)], axis=0
    )


def is_positive(pos_ref, active, blocks):
    pos = expand(pos_ref[...].astype(f32), blocks).astype(jnp.int32)
    item = iota((blocks, B, QT), 1) + lax.axis_index("pa") * B
    return (pos[:, None, :] == item) & active


def scores_kernel(mask_s, pos_ref, q_ref, p_ref, send_ref, logit_ref, top_ref, tot_ref, order, sim_ref):
    blocks = mask_s.shape[0]
    count = list_tasks(mask_s, order)
    top_ref[...] = jnp.zeros_like(top_ref)
    tot_ref[...] = jnp.ones_like(tot_ref)

    @pl.loop(0, (count + 1) // 2)
    def _(step):
        pair = (order[2 * step], order[2 * step + 1])
        qk = pair_queries(q_ref, *pair)
        sim_ref[...] = lax.dot_general(p_ref[...], qk, turned_dims, preferred_element_type=f32)
        for half, k in enumerate(pair):
            part = sim_ref[:, half * QT : (half + 1) * QT].reshape(LP, B, QT)
            top = jnp.max(part, axis=0)
            top_ref[k] = top
            tot_ref[k] = jnp.sum(jnp.exp(part - top[None]), axis=0)

    active = active_blocks(mask_s)
    token_lse = (top_ref[...] + jnp.log(tot_ref[...])).reshape(blocks * B, QT)
    same = (iota((QT, QT), 0) // LQ == iota((QT, QT), 1) // LQ).astype(f32)
    score = (exact_dot(token_lse, same) / LQ).reshape(blocks, B, QT)
    logit = jnp.where(active, score / contrast_temp, very_low)
    logit_ref[...] = logit
    local_top = jnp.max(logit, axis=1, keepdims=True)
    local_total = jnp.sum(jnp.where(active, jnp.exp(logit - local_top), 0.0), axis=1)
    local_pos = jnp.sum(jnp.where(is_positive(pos_ref, active, blocks), logit, 0.0), axis=1)
    rows = [squeeze(x, blocks) for x in (local_top[:, 0, :], local_total, local_pos)]
    rows.append(jnp.zeros((5, blocks * B), f32))
    send_ref[...] = jnp.broadcast_to(jnp.concatenate(rows, axis=0)[None], send_ref.shape)


def grads_kernel(
    mask_s, pos_ref, q_ref, p_ref, stat_ref, logit_ref, top_ref, tot_ref,
    loss_ref, gq_ref, own_ref, send1_ref, send2_ref, send3_ref,
    order, turn_ref, weight_ref, gp_ref, sim_ref, dsim_ref,
):
    blocks = mask_s.shape[0]
    count = list_tasks(mask_s, order)
    turn_ref[...] = p_ref[...].astype(f32).T.astype(bf16)
    tops = stat_ref[:, 0, :]
    glob_top = jnp.max(tops, axis=0, keepdims=True)
    glob_total = jnp.sum(stat_ref[:, 1, :] * jnp.exp(tops - glob_top), axis=0, keepdims=True)
    glob_pos = jnp.sum(stat_ref[:, 2, :], axis=0, keepdims=True)
    loss_ref[...] = glob_top + jnp.log(glob_total) - glob_pos
    active = active_blocks(mask_s)
    wide_top = expand(glob_top, blocks)[:, None, :]
    wide_total = expand(glob_total, blocks)[:, None, :]
    prob = jnp.where(active, jnp.exp(logit_ref[...] - wide_top) / wide_total, 0.0)
    onehot = is_positive(pos_ref, active, blocks).astype(f32)
    weight_ref[...] = (prob - onehot) / (contrast_temp * LQ) / tot_ref[...]
    gp_ref[...] = jnp.zeros_like(gp_ref)
    gq_ref[...] = jnp.zeros_like(gq_ref)

    @pl.loop(0, (count + 1) // 2)
    def _(step):
        pair = (order[2 * step], order[2 * step + 1])
        qk = pair_queries(q_ref, *pair)
        sim_ref[...] = lax.dot_general(p_ref[...], qk, turned_dims, preferred_element_type=f32)
        for half, k in enumerate(pair):
            here = slice(half * QT, (half + 1) * QT)
            part = sim_ref[:, here].reshape(LP, B, QT)
            dsim = jnp.exp(part - top_ref[k][None]) * weight_ref[k][None]
            dsim_ref[:, here] = dsim.astype(bf16).reshape(PT, QT)
        gp_ref[...] += jnp.dot(dsim_ref[...], qk, preferred_element_type=f32)
        turned = jnp.dot(turn_ref[...], dsim_ref[...], preferred_element_type=f32).astype(bf16)
        for half, k in enumerate(pair):
            for j in range(2):
                start = half * QT + j * D
                gq_ref[2 * k + j] = turned[:, start : start + D]

    mine = lax.axis_index("pb")
    piece = PT // 4

    def rows_of(owner):
        return gp_ref[pl.ds(pl.multiple_of(owner * piece, B), piece), :]

    own_ref[...] = rows_of(mine)
    for s, send in ((1, send1_ref), (2, send2_ref), (3, send3_ref)):
        send[...] = rows_of(lax.rem(mine + s, 4)).astype(bf16)


def sum_kernel(own_ref, a_ref, b_ref, c_ref, out_ref):
    total = own_ref[...] + a_ref[...].astype(f32) + b_ref[...].astype(f32) + c_ref[...].astype(f32)
    out_ref[...] = total.astype(bf16)


def place_kernel(own_ref, a_ref, b_ref, c_ref, out_ref):
    mine = lax.axis_index("pb")
    piece = PT // 4
    for s, ref in ((0, own_ref), (1, a_ref), (2, b_ref), (3, c_ref)):
        owner = lax.rem(mine + 4 - s, 4)
        out_ref[pl.ds(pl.multiple_of(owner * piece, B), piece), :] = ref[...].astype(f32)


def rows_kernel(in_ref, out_ref):
    total = in_ref[0].astype(f32)
    for i in range(1, in_ref.shape[0]):
        total += in_ref[i].astype(f32)
    out_ref[...] = total.T


def call(kernel, out, n_in, scalars=0, scratch=(), vmem=48 << 20, flops=0, nbytes=0):
    return pl.pallas_call(
        kernel,
        out_shape=out,
        in_specs=[SMEM if i < scalars else VMEM for i in range(n_in)],
        out_specs=jax.tree.map(lambda _: VMEM, out),
        scratch_shapes=list(scratch),
        compiler_params=pltpu.CompilerParams(vmem_limit_bytes=vmem),
        cost_estimate=pl.CostEstimate(flops=flops, bytes_accessed=nbytes, transcendentals=0),
    )


def turn(x, s):
    return lax.ppermute(x, "pb", [(i, (i + s) % 4) for i in range(4)])


def on_device(queries, passages, pair_mask, positive):
    rows = queries.shape[0]
    blocks = rows // B
    peers = lax.axis_size("pa")
    shape = jax.ShapeDtypeStruct
    flat_q = queries.reshape(rows * LQ, D)
    flat_p = jnp.swapaxes(passages, 0, 1).reshape(PT, D)
    mask = pair_mask.reshape(blocks)
    pos = positive.reshape(1, rows)
    wide = shape((blocks, B, QT), f32)
    order = pltpu.SMEM((blocks,), jnp.int32)
    sim = pltpu.VMEM((PT, 2 * QT), f32)
    send, logit, top, tot = call(
        scores_kernel,
        (shape((peers, 8, rows), f32), wide, wide, wide),
        4,
        1,
        [order, sim],
        flops=5_000_000_000,
        nbytes=3_000_000,
    )(mask, pos, flat_q, flat_p)
    stats = lax.all_to_all(send, "pa", 0, 0, tiled=True)
    piece = shape((PT // 4, D), bf16)
    loss, gq, own, send1, send2, send3 = call(
        grads_kernel,
        (shape((1, rows), f32), shape((peers, D, 4 * LQ), bf16), shape((PT // 4, D), f32), piece, piece, piece),
        8,
        1,
        [
            order,
            pltpu.VMEM((D, PT), bf16),
            pltpu.VMEM((blocks, B, QT), f32),
            pltpu.VMEM((PT, D), f32),
            sim,
            pltpu.VMEM((PT, 2 * QT), bf16),
        ],
        flops=10_000_000_000,
        nbytes=5_000_000,
    )(mask, pos, flat_q, flat_p, stats, logit, top, tot)
    got = [turn(x, s) for x, s in ((send1, 1), (send2, 2), (send3, 3))]
    gq_terms = lax.all_to_all(gq, "pa", 0, 0, tiled=True)
    mine = call(sum_kernel, piece, 4, nbytes=1_000_000)(own, *got)
    others = [turn(mine, s) for s in (1, 2, 3)]
    flat = call(place_kernel, shape((PT, D), f32), 4, nbytes=1_000_000)(mine, *others)
    grad_p = jnp.swapaxes(flat.reshape(LP, B, D), 0, 1)
    grad_q = call(rows_kernel, shape((4 * LQ, D), f32), 1, nbytes=1_000_000)(gq_terms)
    loss_rows = lax.dynamic_slice_in_dim(loss[0], lax.axis_index("pa") * 4, 4, 0)
    return loss_rows, grad_q.reshape(4, LQ, D), grad_p


def solution(mesh):
    placed = (P("pb", None, None), P("pa", None, None), P("pb", "pa"), P("pb"))
    return jax.shard_map(
        on_device,
        mesh=mesh,
        in_specs=placed,
        out_specs=(P(("pb", "pa")), P(("pb", "pa"), None, None), P("pa", None, None)),
        check_vma=False,
    )
```

```python
import jax
import jax.numpy as jnp
from jax import lax
from jax.experimental import pallas as pl
from jax.experimental.pallas import tpu as pltpu
from jax.sharding import PartitionSpec as P

very_low = -1e30
contrast_temp = 0.05
safe_low, safe_high = 1e-12, 1e12
kept_pairs = 5
f32, bf16 = jnp.float32, jnp.bfloat16
VMEM = pl.BlockSpec(memory_space=pltpu.VMEM)
SMEM = pl.BlockSpec(memory_space=pltpu.SMEM)
ANY = pl.BlockSpec(memory_space=pl.ANY)
B, LQ, LP, D = 8, 32, 180, 128
QT = B * LQ
PT = B * LP
turned_dims = (((1,), (1,)), ((), ()))


def iota(shape, dim):
    return lax.broadcasted_iota(jnp.int32, shape, dim)


def exact_dot(a, b):
    return jnp.dot(a, b, precision=lax.Precision.HIGHEST, preferred_element_type=f32)


def expand(row, blocks):
    count = blocks * B
    own = iota((blocks, count), 1) // B == iota((blocks, count), 0)
    pick = (iota((count, QT), 0) % B == iota((count, QT), 1) // LQ).astype(f32)
    return exact_dot(jnp.where(own, row, 0.0), pick)


def squeeze(wides, blocks):
    count = blocks * B
    pick = (iota((QT, count), 0) == LQ * (iota((QT, count), 1) % B)).astype(f32)
    own = iota((blocks, count), 1) // B == iota((blocks, count), 0)
    picked = exact_dot(jnp.concatenate(wides, axis=0), pick).reshape(len(wides), blocks, count)
    return [jnp.sum(jnp.where(own, x, 0.0), axis=0, keepdims=True) for x in picked]


def list_tasks(mask_s, order):
    blocks = mask_s.shape[0]
    count = jnp.int32(0)
    for wanted in (True, False):
        for k in range(blocks):
            here = (mask_s[k] > 0) == wanted

            @pl.when(here)
            def _(k=k, count=count):
                order[count] = k

            count = count + here.astype(jnp.int32)
        if wanted:
            active = count
    return active


def active_blocks(mask_s):
    blocks = mask_s.shape[0]
    return jnp.stack([jnp.full((B, QT), mask_s[k], jnp.int32) for k in range(blocks)]) > 0


def is_positive(pos_ref, active, blocks):
    pos = expand(pos_ref[...].astype(f32), blocks).astype(jnp.int32)
    item = iota((blocks, B, QT), 1) + lax.axis_index("pa") * B
    return (pos[:, None, :] == item) & active


def block_rows(q_ref, k):
    return q_ref[pl.ds(pl.multiple_of(k * QT, QT), QT), :]


def fetch_all(pairs, sems):
    fetches = [pltpu.make_async_copy(src, dst, sems.at[i]) for i, (src, dst) in enumerate(pairs)]
    for fetch in fetches:
        fetch.start()
    return [fetch.wait for fetch in fetches]


def task_sim(p_ref, q_ref, k):
    return lax.dot_general(p_ref[...], block_rows(q_ref, k), turned_dims, preferred_element_type=f32)


def scores_kernel(
    mask_hbm, pos_hbm, q_hbm, p_hbm,
    send_ref, logit_ref, onehot_ref, top_ref, tot_ref, kept_hbm,
    mask_s, pos_ref, q_ref, p_ref, order, sim_ref, kept_ref, sems, kept_sems,
):
    blocks = mask_s.shape[0]
    pairs = ((mask_hbm, mask_s), (pos_hbm, pos_ref), (p_hbm, p_ref), (q_hbm, q_ref))
    mask_wait, pos_wait, p_wait, q_wait = fetch_all(pairs, sems)
    top_ref[...] = jnp.zeros_like(top_ref)
    tot_ref[...] = jnp.ones_like(tot_ref)
    mask_wait()
    count = list_tasks(mask_s, order)
    steps = (count + 1) // 2
    kept_steps = jnp.minimum(steps, kept_pairs)
    active = active_blocks(mask_s)
    pos_wait()
    positive = is_positive(pos_ref, active, blocks)
    onehot_ref[...] = positive.astype(f32)
    p_wait()
    q_wait()

    def keep(task):
        return pltpu.make_async_copy(kept_ref.at[task], kept_hbm.at[task], kept_sems.at[task])

    def no_shift(task):
        k = order[task]
        scaled = jnp.exp(task_sim(p_ref, q_ref, k))
        tot_ref[k] = jnp.sum(scaled.reshape(LP, B, QT), axis=0)
        return scaled

    @pl.loop(0, kept_steps)
    def _(step):
        for half in range(2):
            kept_ref[2 * step + half] = no_shift(2 * step + half)
        for half in range(2):
            keep(2 * step + half).start()

    @pl.loop(kept_steps, steps)
    def _(step):
        for half in range(2):
            no_shift(2 * step + half)

    safe = (jnp.min(tot_ref[...]) > safe_low) & (jnp.max(tot_ref[...]) < safe_high)

    @pl.when(jnp.logical_not(safe))
    def _():
        @pl.loop(0, 2 * kept_steps)
        def _(task):
            keep(task).wait()

        @pl.loop(0, 2 * steps)
        def _(task):
            k = order[task]
            sim_ref[...] = task_sim(p_ref, q_ref, k)
            sim = sim_ref[...].reshape(LP, B, QT)
            top = jnp.max(sim, axis=0)
            scaled = jnp.exp(sim - top[None])
            top_ref[k] = top
            tot_ref[k] = jnp.sum(scaled, axis=0)

            @pl.when(task < 2 * kept_steps)
            def _():
                kept_ref[task] = scaled.reshape(PT, QT)
                keep(task).start()

    token_lse = (top_ref[...] + jnp.log(tot_ref[...])).reshape(blocks * B, QT)
    same = (iota((QT, QT), 0) // LQ == iota((QT, QT), 1) // LQ).astype(f32)
    score = (exact_dot(token_lse, same) / LQ).reshape(blocks, B, QT)
    logit = jnp.where(active, score / contrast_temp, very_low)
    logit_ref[...] = logit
    local_top = jnp.max(logit, axis=1, keepdims=True)
    local_total = jnp.sum(jnp.where(active, jnp.exp(logit - local_top), 0.0), axis=1)
    local_pos = jnp.sum(jnp.where(positive, logit, 0.0), axis=1)
    rows = squeeze((local_top[:, 0, :], local_total, local_pos), blocks)
    rows.append(jnp.zeros((5, blocks * B), f32))
    send_ref[...] = jnp.broadcast_to(jnp.concatenate(rows, axis=0)[None], send_ref.shape)

    @pl.loop(0, 2 * kept_steps)
    def _(task):
        keep(task).wait()


def grads_kernel(
    mask_hbm, stat_ref, logit_hbm, onehot_hbm, top_hbm, tot_hbm, q_hbm, p_hbm, turn_hbm, kept_hbm,
    loss_ref, gq_ref, own_ref, send1_ref, send2_ref, send3_ref,
    mask_s, logit_ref, onehot_ref, top_ref, tot_ref, q_ref, p_ref, turn_ref, kept_ref,
    order, weight_ref, gp_ref, sim_ref, dsim_ref, sems, kept_sems,
):
    blocks = mask_s.shape[0]
    ins = (mask_hbm, logit_hbm, onehot_hbm, top_hbm, tot_hbm, q_hbm, p_hbm, turn_hbm)
    refs = (mask_s, logit_ref, onehot_ref, top_ref, tot_ref, q_ref, p_ref, turn_ref)
    waits = fetch_all(zip(ins, refs), sems)

    def kept(task):
        return pltpu.make_async_copy(kept_hbm.at[task], kept_ref.at[task], kept_sems.at[task])

    waits[0]()
    count = list_tasks(mask_s, order)
    steps = (count + 1) // 2
    kept_steps = jnp.minimum(steps, kept_pairs)
    gp_ref[...] = jnp.zeros_like(gp_ref)
    tops = stat_ref[:, 0, :]
    glob_top = jnp.max(tops, axis=0, keepdims=True)
    glob_total = jnp.sum(stat_ref[:, 1, :] * jnp.exp(tops - glob_top), axis=0, keepdims=True)
    glob_pos = jnp.sum(stat_ref[:, 2, :], axis=0, keepdims=True)
    loss_ref[...] = glob_top + jnp.log(glob_total) - glob_pos
    wide_top = expand(glob_top, blocks)[:, None, :]
    wide_total = expand(glob_total, blocks)[:, None, :]
    for wait in waits[1:]:
        wait()

    @pl.loop(0, 2 * kept_steps)
    def _(task):
        kept(task).start()

    active = logit_ref[...] > very_low / 2
    prob = jnp.where(active, jnp.exp(logit_ref[...] - wide_top) / wide_total, 0.0)
    weight_ref[...] = (prob - onehot_ref[...]) / (contrast_temp * LQ) / tot_ref[...]

    def grads(step, scaled_of):
        pair = (order[2 * step], order[2 * step + 1])
        for half, k in enumerate(pair):
            scaled = scaled_of(half, k).reshape(LP, B, QT)
            dsim = (scaled * weight_ref[k][None]).astype(bf16)
            dsim_ref[:, half * QT : (half + 1) * QT] = dsim.reshape(PT, QT)
        qk = jnp.concatenate([block_rows(q_ref, k) for k in pair], axis=0)
        gp_ref[...] += jnp.dot(dsim_ref[...], qk, preferred_element_type=f32)
        turned = jnp.dot(turn_ref[...], dsim_ref[...], preferred_element_type=f32).astype(bf16)
        for half, k in enumerate(pair):
            for j in range(2):
                start = half * QT + j * D
                gq_ref[2 * k + j] = turned[:, start : start + D]

    @pl.loop(kept_steps, steps)
    def _(step):
        both = jnp.concatenate([block_rows(q_ref, order[2 * step + half]) for half in range(2)], axis=0)
        sim_ref[...] = lax.dot_general(p_ref[...], both, turned_dims, preferred_element_type=f32)

        def again(half, k):
            sim = sim_ref[:, half * QT : (half + 1) * QT].reshape(LP, B, QT)
            return jnp.exp(sim - top_ref[k][None])

        grads(step, again)

    @pl.loop(0, kept_steps)
    def _(step):
        kept(2 * step).wait()
        kept(2 * step + 1).wait()
        grads(step, lambda half, k: kept_ref[2 * step + half])

    @pl.loop(2 * steps, blocks)
    def _(task):
        k = order[task]
        for j in range(2):
            gq_ref[2 * k + j] = jnp.zeros((D, 4 * LQ), bf16)

    mine = lax.axis_index("pb")
    piece = PT // 4

    def rows_of(owner):
        return gp_ref[pl.ds(pl.multiple_of(owner * piece, B), piece), :]

    own_ref[...] = rows_of(mine)
    for s, send in ((1, send1_ref), (2, send2_ref), (3, send3_ref)):
        send[...] = rows_of(lax.rem(mine + s, 4)).astype(bf16)


def turn_kernel(p_ref, out_ref):
    out_ref[...] = p_ref[...].astype(f32).T.astype(bf16)


def sum_kernel(own_ref, a_ref, b_ref, c_ref, out_ref):
    total = own_ref[...] + a_ref[...].astype(f32) + b_ref[...].astype(f32) + c_ref[...].astype(f32)
    out_ref[...] = total.astype(bf16)


def last_kernel(own_ref, a_ref, b_ref, c_ref, terms_ref, gp_ref, gq_ref):
    mine = lax.axis_index("pb")
    piece = PT // 4
    for s, ref in ((0, own_ref), (1, a_ref), (2, b_ref), (3, c_ref)):
        owner = lax.rem(mine + 4 - s, 4)
        gp_ref[pl.ds(pl.multiple_of(owner * piece, B), piece), :] = ref[...].astype(f32)
    total = terms_ref[0].astype(f32)
    for i in range(1, terms_ref.shape[0]):
        total += terms_ref[i].astype(f32)
    gq_ref[...] = total.T


def in_hbm(x):
    return pltpu.with_memory_space_constraint(x, pltpu.HBM)


def call(kernel, out, specs, scratch=(), outs=None, vmem=40 << 20, flops=0, nbytes=0):
    return pl.pallas_call(
        kernel,
        out_shape=out,
        in_specs=list(specs),
        out_specs=outs or jax.tree.map(lambda _: VMEM, out),
        scratch_shapes=list(scratch),
        compiler_params=pltpu.CompilerParams(vmem_limit_bytes=vmem),
        cost_estimate=pl.CostEstimate(flops=flops, bytes_accessed=nbytes, transcendentals=0),
    )


def turn(x, s):
    return lax.ppermute(x, "pb", [(i, (i + s) % 4) for i in range(4)])


def on_device(queries, passages, pair_mask, positive):
    rows = queries.shape[0]
    blocks = rows // B
    peers = lax.axis_size("pa")
    shape = jax.ShapeDtypeStruct
    flat_q = queries.reshape(rows * LQ, D)
    flat_p = jnp.swapaxes(passages, 0, 1).reshape(PT, D)
    mask = pair_mask.reshape(blocks)
    pos = positive.reshape(1, rows)
    wide = shape((blocks, B, QT), f32)
    ints = pltpu.SMEM((blocks,), jnp.int32)
    vmem = pltpu.VMEM
    wide_ref, q_ref, p_ref = vmem((blocks, B, QT), f32), vmem((rows * LQ, D), bf16), vmem((PT, D), bf16)
    kept_ref = vmem((2 * kept_pairs, PT, QT), f32)
    kept_sems = pltpu.SemaphoreType.DMA((2 * kept_pairs,))
    mask, pos, flat_q, flat_p = (in_hbm(x) for x in (mask, pos, flat_q, flat_p))
    wide = pltpu.HBM((blocks, B, QT), f32)
    send, logit, onehot, top, tot, kept = call(
        scores_kernel,
        (shape((peers, 8, rows), f32), wide, wide, wide, wide, pltpu.HBM(kept_ref.shape, f32)),
        (ANY,) * 4,
        [
            ints,
            vmem((1, rows), jnp.int32),
            q_ref,
            p_ref,
            ints,
            vmem((PT, QT), f32),
            kept_ref,
            pltpu.SemaphoreType.DMA((4,)),
            kept_sems,
        ],
        outs=(VMEM,) * 5 + (ANY,),
        flops=2_000_000_000,
        nbytes=3_000_000,
    )(mask, pos, flat_q, flat_p)
    stats = lax.all_to_all(send, "pa", 0, 0, tiled=True)
    flat_p_after, _ = lax.optimization_barrier((flat_p, tot))
    turned_p = call(turn_kernel, pltpu.HBM((D, PT), bf16), (VMEM,), nbytes=1_000_000)(flat_p_after)
    piece = shape((PT // 4, D), bf16)
    ins = (logit, onehot, top, tot, flat_q, flat_p, turned_p, kept)
    loss, gq, own, send1, send2, send3 = call(
        grads_kernel,
        (shape((1, rows), f32), shape((peers, D, 4 * LQ), bf16), shape((PT // 4, D), f32), piece, piece, piece),
        (ANY, VMEM) + (ANY,) * 8,
        [
            ints,
            wide_ref,
            wide_ref,
            wide_ref,
            wide_ref,
            q_ref,
            p_ref,
            vmem((D, PT), bf16),
            kept_ref,
            ints,
            wide_ref,
            vmem((PT, D), f32),
            vmem((PT, 2 * QT), f32),
            vmem((PT, 2 * QT), bf16),
            pltpu.SemaphoreType.DMA((8,)),
            kept_sems,
        ],
        flops=5_000_000_000,
        nbytes=5_000_000,
    )(mask, stats, *(in_hbm(x) for x in ins))
    got = [turn(x, s) for x, s in ((send1, 1), (send2, 2), (send3, 3))]
    gq_terms = lax.all_to_all(gq, "pa", 0, 0, tiled=True)
    mine = call(sum_kernel, piece, (VMEM,) * 4, nbytes=1_000_000)(own, *got)
    others = [turn(mine, s) for s in (1, 2, 3)]
    flat, grad_q = call(
        last_kernel, (shape((PT, D), f32), shape((4 * LQ, D), f32)), (VMEM,) * 5, nbytes=2_000_000
    )(mine, *others, gq_terms)
    grad_p = jnp.swapaxes(flat.reshape(LP, B, D), 0, 1)
    loss_rows = lax.dynamic_slice_in_dim(loss[0], lax.axis_index("pa") * 4, 4, 0)
    return loss_rows, grad_q.reshape(4, LQ, D), grad_p


def solution(mesh):
    placed = (P("pb", None, None), P("pa", None, None), P("pb", "pa"), P("pb"))
    return jax.shard_map(
        on_device,
        mesh=mesh,
        in_specs=placed,
        out_specs=(P(("pb", "pa")), P(("pb", "pa"), None, None), P("pa", None, None)),
        check_vma=False,
    )
```

```python
import jax
import jax.numpy as jnp
from jax import lax
from jax.experimental import pallas as pl
from jax.experimental.pallas import tpu as pltpu
from jax.sharding import PartitionSpec as P

very_low = -1e30
contrast_temp = 0.05
safe_low, safe_high = 1e-12, 1e12
f32, bf16 = jnp.float32, jnp.bfloat16
VMEM = pl.BlockSpec(memory_space=pltpu.VMEM)
ANY = pl.BlockSpec(memory_space=pl.ANY)
B, LQ, LP, D = 8, 32, 180, 128
QT = B * LQ
PT = B * LP
GROUP = 4
turned_dims = (((1,), (1,)), ((), ()))


def iota(shape, dim):
    return lax.broadcasted_iota(jnp.int32, shape, dim)


def exact_dot(a, b):
    return jnp.dot(a, b, precision=lax.Precision.HIGHEST, preferred_element_type=f32)


def own_lanes(blocks):
    return iota((blocks, B, blocks * B), 2) // B == iota((blocks, B, blocks * B), 0)


def pack_means(wide):
    blocks = wide.shape[0]
    count = blocks * B
    pick = (iota((QT, count), 0) // LQ == iota((QT, count), 1) % B).astype(f32)
    sums = exact_dot(wide.reshape(count, QT), pick).reshape(blocks, B, count)
    return jnp.sum(jnp.where(own_lanes(blocks), sums, 0.0), axis=0) / LQ


def unpack(packed):
    count = packed.shape[1]
    blocks = count // B
    pick = (iota((count, QT), 0) % B == iota((count, QT), 1) // LQ).astype(f32)
    spread = jnp.where(own_lanes(blocks), packed[None], 0.0).reshape(count, count)
    return exact_dot(spread, pick).reshape(blocks, B, QT)


def list_tasks(mask_s, order):
    blocks = mask_s.shape[0]
    count = jnp.int32(0)
    for wanted in (True, False):
        for k in range(blocks):
            here = (mask_s[k] > 0) == wanted

            @pl.when(here)
            def _(k=k, count=count):
                order[count] = k

            count = count + here.astype(jnp.int32)
        if wanted:
            active = count
    return active


def block_rows(q_ref, k):
    return q_ref[pl.ds(pl.multiple_of(k * QT, QT), QT), :]


def fetch_all(pairs, sems):
    fetches = [pltpu.make_async_copy(src, dst, sems.at[i]) for i, (src, dst) in enumerate(pairs)]
    for fetch in fetches:
        fetch.start()
    return [fetch.wait for fetch in fetches]


def task_sim(p_ref, q_ref, k):
    return lax.dot_general(p_ref[...], block_rows(q_ref, k), turned_dims, preferred_element_type=f32)


def scores_kernel(mask_hbm, pos_hbm, q_hbm, p_hbm, send_ref, logit_ref, tot_ref, q_ref, p_ref, *rest):
    blocks = tot_ref.shape[0]
    groups = blocks // GROUP
    scaled_refs, (mask_s, pos_ref, order, top_ref, sim_ref, sems) = rest[:groups], rest[groups:]
    pairs = ((mask_hbm, mask_s), (pos_hbm, pos_ref), (p_hbm, p_ref), (q_hbm, q_ref))
    mask_wait, pos_wait, p_wait, q_wait = fetch_all(pairs, sems)
    top_ref[...] = jnp.zeros_like(top_ref)
    tot_ref[...] = jnp.ones_like(tot_ref)
    mask_wait()
    count = list_tasks(mask_s, order)
    pos_wait()
    p_wait()
    q_wait()
    for group, scaled_ref in enumerate(scaled_refs):

        @pl.when(count > group * GROUP)
        def _(group=group, scaled_ref=scaled_ref):
            for i in range(GROUP):
                k = order[group * GROUP + i]
                scaled = jnp.exp(task_sim(p_ref, q_ref, k))
                scaled_ref[i] = scaled
                tot_ref[k] = jnp.sum(scaled.reshape(LP, B, QT), axis=0)

    safe = (jnp.min(tot_ref[...]) > safe_low) & (jnp.max(tot_ref[...]) < safe_high)

    @pl.when(jnp.logical_not(safe))
    def _():
        for group, scaled_ref in enumerate(scaled_refs):

            @pl.when(count > group * GROUP)
            def _(group=group, scaled_ref=scaled_ref):
                @pl.loop(0, GROUP)
                def _(i):
                    k = order[group * GROUP + i]
                    sim_ref[...] = task_sim(p_ref, q_ref, k)
                    sim = sim_ref[...].reshape(LP, B, QT)
                    top = jnp.max(sim, axis=0)
                    scaled = jnp.exp(sim - top[None])
                    top_ref[k] = top
                    tot_ref[k] = jnp.sum(scaled, axis=0)
                    scaled_ref[i] = scaled.reshape(PT, QT)

    lane_block = iota((B, blocks * B), 1) // B
    active = jnp.zeros((B, blocks * B), jnp.int32)
    for k in range(blocks):
        active = jnp.where(lane_block == k, mask_s[k], active)
    active = active > 0
    score = pack_means(top_ref[...] + jnp.log(tot_ref[...]))
    logit = jnp.where(active, score / contrast_temp, very_low)
    logit_ref[...] = logit
    positive = (pos_ref[...] == iota(logit.shape, 0) + lax.axis_index("pa") * B) & active
    local_top = jnp.max(logit, axis=0, keepdims=True)
    scaled = jnp.where(active, jnp.exp(logit - local_top), 0.0)
    local_total = jnp.sum(scaled, axis=0, keepdims=True)
    local_pos = jnp.sum(jnp.where(positive, logit, 0.0), axis=0, keepdims=True)
    row = iota(logit.shape, 0)
    send = jnp.where(row == 0, local_top, jnp.where(row == 1, local_total, local_pos))
    send_ref[...] = jnp.where(row < 3, send, 0.0)


def merged(*stats):
    row = iota(stats[0].shape, 0)
    top = stats[0][:1]
    for x in stats[1:]:
        top = jnp.maximum(top, x[:1])
    total = sum(x * jnp.where(row == 1, jnp.exp(x[:1] - top), 1.0) for x in stats)
    return jnp.where(row == 0, top, total)


def grads_kernel(
    mask_hbm, pos_ref, stat0_ref, stat1_ref, stat2_ref, stat3_ref, logit_ref, tot_ref, q_ref, turn_ref, *rest
):
    blocks = tot_ref.shape[0]
    groups = blocks // GROUP
    scaled_refs, rest = rest[:groups], rest[groups:]
    loss_ref, gq_ref, own_ref, send1_ref, send2_ref, send3_ref, *rest = rest
    mask_s, order, weight_ref, gp_ref, dsim_ref, sem = rest
    fetch = pltpu.make_async_copy(mask_hbm, mask_s, sem)
    fetch.start()
    stat = merged(stat0_ref[...], stat1_ref[...], stat2_ref[...], stat3_ref[...])
    glob_top, glob_total, glob_pos = stat[:1], stat[1:2], stat[2:3]
    loss_ref[...] = glob_top + jnp.log(glob_total) - glob_pos
    logit = logit_ref[...]
    active = logit > very_low / 2
    positive = (pos_ref[...] == iota(logit.shape, 0) + lax.axis_index("pa") * B) & active
    prob = jnp.where(active, jnp.exp(logit - glob_top) / glob_total, 0.0)
    coef = (prob - positive.astype(f32)) / (contrast_temp * LQ)
    weight_ref[...] = unpack(coef) / tot_ref[...]
    gp_ref[...] = jnp.zeros_like(gp_ref)
    fetch.wait()
    count = list_tasks(mask_s, order)
    for group, scaled_ref in enumerate(scaled_refs):

        @pl.when(count > group * GROUP)
        def _(group=group, scaled_ref=scaled_ref):
            tasks = [order[group * GROUP + i] for i in range(GROUP)]
            for i, k in enumerate(tasks):
                dsim = (scaled_ref[i].reshape(LP, B, QT) * weight_ref[k][None]).astype(bf16)
                dsim_ref[:, i * QT : (i + 1) * QT] = dsim.reshape(PT, QT)
            queries = jnp.concatenate([block_rows(q_ref, k) for k in tasks], axis=0)
            gp_ref[...] += jnp.dot(dsim_ref[...], queries, preferred_element_type=f32)
            turned = jnp.dot(turn_ref[...], dsim_ref[...], preferred_element_type=f32).astype(bf16)
            for i, k in enumerate(tasks):
                for j in range(2):
                    start = i * QT + j * D
                    gq_ref[2 * k + j] = turned[:, start : start + D]

        @pl.when(count <= group * GROUP)
        def _(group=group):
            for i in range(GROUP):
                for j in range(2):
                    gq_ref[2 * order[group * GROUP + i] + j] = jnp.zeros((D, 4 * LQ), bf16)

    mine = lax.axis_index("pb")
    piece = PT // 4

    def rows_of(owner):
        return gp_ref[pl.ds(pl.multiple_of(owner * piece, B), piece), :]

    own_ref[...] = rows_of(mine)
    for s, send in ((1, send1_ref), (2, send2_ref), (3, send3_ref)):
        send[...] = rows_of(lax.rem(mine + s, 4)).astype(bf16)


def turn_kernel(p_ref, out_ref):
    out_ref[...] = p_ref[...].astype(f32).T.astype(bf16)


def sum_kernel(own_ref, a_ref, b_ref, c_ref, out_ref):
    total = own_ref[...] + a_ref[...].astype(f32) + b_ref[...].astype(f32) + c_ref[...].astype(f32)
    out_ref[...] = total.astype(bf16)


def last_kernel(loss_ref, own_ref, a_ref, b_ref, c_ref, terms_ref, gp_ref, gq_ref, rows_ref):
    mine = lax.axis_index("pb")
    piece = PT // 4
    for s, ref in ((0, own_ref), (1, a_ref), (2, b_ref), (3, c_ref)):
        owner = lax.rem(mine + 4 - s, 4)
        gp_ref[pl.ds(pl.multiple_of(owner * piece, B), piece), :] = ref[...].astype(f32)
    total = terms_ref[0].astype(f32)
    for i in range(1, terms_ref.shape[0]):
        total += terms_ref[i].astype(f32)
    gq_ref[...] = total.T
    count, own = loss_ref.shape[1], rows_ref.shape[1]
    pick = iota((count, own), 0) == iota((count, own), 1) + own * lax.axis_index("pa")
    rows_ref[...] = exact_dot(loss_ref[...], pick.astype(f32))


def in_hbm(x):
    return pltpu.with_memory_space_constraint(x, pltpu.HBM)


def call(kernel, out, specs, scratch=(), vmem=16 << 20, flops=0, nbytes=0):
    return pl.pallas_call(
        kernel,
        out_shape=out,
        in_specs=list(specs),
        out_specs=jax.tree.map(lambda _: VMEM, out),
        scratch_shapes=list(scratch),
        compiler_params=pltpu.CompilerParams(vmem_limit_bytes=vmem),
        cost_estimate=pl.CostEstimate(flops=flops, bytes_accessed=nbytes, transcendentals=0),
    )


def turn(x, s):
    return lax.ppermute(x, "pb", [(i, (i + s) % 4) for i in range(4)])


def turn_digit(x, s, unit):
    def to(i):
        return i + unit * ((i // unit + s) % 4 - i // unit % 4)

    return lax.ppermute(x, "pa", [(i, to(i)) for i in range(lax.axis_size("pa"))])


def on_device(queries, passages, pair_mask, positive):
    rows = queries.shape[0]
    blocks = rows // B
    groups = blocks // GROUP
    peers = lax.axis_size("pa")
    own_rows = rows // peers
    shape = jax.ShapeDtypeStruct
    flat_q = queries.reshape(rows * LQ, D)
    flat_p = jnp.swapaxes(passages, 0, 1).reshape(PT, D)
    mask = pair_mask.reshape(blocks)
    pos = positive.reshape(1, rows)
    ints = pltpu.SMEM((blocks,), jnp.int32)
    mask, flat_q, flat_p = (in_hbm(x) for x in (mask, flat_q, flat_p))
    wide = shape((blocks, B, QT), f32)
    packed = shape((B, rows), f32)
    send, logit, tot, near_q, near_p, *scaled = call(
        scores_kernel,
        (
            packed,
            packed,
            wide,
            shape((rows * LQ, D), bf16),
            shape((PT, D), bf16),
            *(shape((GROUP, PT, QT), f32),) * groups,
        ),
        (ANY,) * 4,
        [
            ints,
            pltpu.VMEM((1, rows), jnp.int32),
            ints,
            pltpu.VMEM((blocks, B, QT), f32),
            pltpu.VMEM((PT, QT), f32),
            pltpu.SemaphoreType.DMA((4,)),
        ],
        flops=2_000_000_000,
        nbytes=3_000_000,
    )(mask, in_hbm(pos), flat_q, flat_p)
    stat = merged(send, lax.ppermute(send, "pa", [(i, i ^ 1) for i in range(peers)]))
    stat = merged(stat, *(turn_digit(stat, s, 2) for s in (1, 2, 3)))
    stats = (stat, *(turn_digit(stat, s, 8) for s in (3, 2, 1)))
    turned_p = call(turn_kernel, shape((D, PT), bf16), (VMEM,), nbytes=100_000)(near_p)
    piece = shape((PT // 4, D), bf16)
    loss, gq, own, send1, send2, send3 = call(
        grads_kernel,
        (shape((1, rows), f32), shape((peers, D, own_rows * LQ), bf16), shape((PT // 4, D), f32), piece, piece, piece),
        (ANY,) + (VMEM,) * (9 + groups),
        [
            ints,
            ints,
            pltpu.VMEM((blocks, B, QT), f32),
            pltpu.VMEM((PT, D), f32),
            pltpu.VMEM((PT, GROUP * QT), bf16),
            pltpu.SemaphoreType.DMA,
        ],
        flops=5_000_000_000,
        nbytes=5_000_000,
    )(mask, pos, *stats, logit, tot, near_q, turned_p, *scaled)
    sends = {1: send1, 2: send2, 3: send3}
    got = [turn(sends[s], s) for s in (1, 2, 3)]
    gq_terms = lax.all_to_all(gq, "pa", 0, 0, tiled=True)
    mine = call(sum_kernel, piece, (VMEM,) * 4, nbytes=1_000_000)(own, *got)
    others = [turn(mine, s) for s in (1, 2, 3)]
    flat, grad_q, loss_rows = call(
        last_kernel,
        (shape((PT, D), f32), shape((own_rows * LQ, D), f32), shape((1, own_rows), f32)),
        (VMEM,) * 6,
        nbytes=2_000_000,
    )(loss, mine, *others, gq_terms)
    grad_p = jnp.swapaxes(flat.reshape(LP, B, D), 0, 1)
    return loss_rows.reshape(own_rows), grad_q.reshape(own_rows, LQ, D), grad_p


def solution(mesh):
    placed = (P("pb", None, None), P("pa", None, None), P("pb", "pa"), P("pb"))
    return jax.shard_map(
        on_device,
        mesh=mesh,
        in_specs=placed,
        out_specs=(P(("pb", "pa")), P(("pb", "pa"), None, None), P("pa", None, None)),
        check_vma=False,
    )
```

```python
import jax
import jax.numpy as jnp
from jax import lax
from jax.experimental import pallas as pl
from jax.experimental.pallas import tpu as pltpu
from jax.sharding import PartitionSpec as P

very_low = -1e30
contrast_temp = 0.05
safe_low, safe_high = 1e-12, 1e12
f32, bf16 = jnp.float32, jnp.bfloat16
VMEM = pl.BlockSpec(memory_space=pltpu.VMEM)
ANY = pl.BlockSpec(memory_space=pl.ANY)
B, LQ, LP, D = 8, 32, 180, 128
QT = B * LQ
PT = B * LP
GROUP = 4
turned_dims = (((1,), (1,)), ((), ()))


def iota(shape, dim):
    return lax.broadcasted_iota(jnp.int32, shape, dim)


def exact_dot(a, b):
    return jnp.dot(a, b, precision=lax.Precision.HIGHEST, preferred_element_type=f32)


def own_lanes(blocks):
    return iota((blocks, B, blocks * B), 2) // B == iota((blocks, B, blocks * B), 0)


def pack_means(wide):
    blocks = wide.shape[0]
    count = blocks * B
    pick = (iota((QT, count), 0) // LQ == iota((QT, count), 1) % B).astype(f32)
    sums = exact_dot(wide.reshape(count, QT), pick).reshape(blocks, B, count)
    return jnp.sum(jnp.where(own_lanes(blocks), sums, 0.0), axis=0) / LQ


def unpack(packed):
    count = packed.shape[1]
    blocks = count // B
    pick = (iota((count, QT), 0) % B == iota((count, QT), 1) // LQ).astype(f32)
    spread = jnp.where(own_lanes(blocks), packed[None], 0.0).reshape(count, count)
    return exact_dot(spread, pick).reshape(blocks, B, QT)


def list_tasks(mask_s, order):
    blocks = mask_s.shape[0]
    count = jnp.int32(0)
    for wanted in (True, False):
        for k in range(blocks):
            here = (mask_s[k] > 0) == wanted

            @pl.when(here)
            def _(k=k, count=count):
                order[count] = k

            count = count + here.astype(jnp.int32)
        if wanted:
            active = count
    return active


def block_rows(q_ref, k):
    return q_ref[pl.ds(pl.multiple_of(k * QT, QT), QT), :]


def fetch_all(pairs, sems):
    fetches = [pltpu.make_async_copy(src, dst, sems.at[i]) for i, (src, dst) in enumerate(pairs)]
    for fetch in fetches:
        fetch.start()
    return [fetch.wait for fetch in fetches]


def task_sim(p_ref, q_ref, k):
    return lax.dot_general(p_ref[...], block_rows(q_ref, k), turned_dims, preferred_element_type=f32)


def scores_kernel(mask_hbm, pos_hbm, q_hbm, p_hbm, send_ref, logit_ref, tot_ref, q_ref, p_ref, *rest):
    blocks = tot_ref.shape[0]
    groups = blocks // GROUP
    scaled_refs, (mask_s, pos_ref, order, top_ref, sim_ref, sems) = rest[:groups], rest[groups:]
    pairs = ((mask_hbm, mask_s), (pos_hbm, pos_ref), (p_hbm, p_ref), (q_hbm, q_ref))
    mask_wait, pos_wait, p_wait, q_wait = fetch_all(pairs, sems)
    top_ref[...] = jnp.zeros_like(top_ref)
    tot_ref[...] = jnp.ones_like(tot_ref)
    mask_wait()
    count = list_tasks(mask_s, order)
    pos_wait()
    p_wait()
    q_wait()
    for group, scaled_ref in enumerate(scaled_refs):

        @pl.when(count > group * GROUP)
        def _(group=group, scaled_ref=scaled_ref):
            for i in range(GROUP):
                k = order[group * GROUP + i]
                scaled = jnp.exp(task_sim(p_ref, q_ref, k))
                scaled_ref[i] = scaled
                tot_ref[k] = jnp.sum(scaled.reshape(LP, B, QT), axis=0)

    safe = (jnp.min(tot_ref[...]) > safe_low) & (jnp.max(tot_ref[...]) < safe_high)

    @pl.when(jnp.logical_not(safe))
    def _():
        for group, scaled_ref in enumerate(scaled_refs):

            @pl.when(count > group * GROUP)
            def _(group=group, scaled_ref=scaled_ref):
                @pl.loop(0, GROUP)
                def _(i):
                    k = order[group * GROUP + i]
                    sim_ref[...] = task_sim(p_ref, q_ref, k)
                    sim = sim_ref[...].reshape(LP, B, QT)
                    top = jnp.max(sim, axis=0)
                    scaled = jnp.exp(sim - top[None])
                    top_ref[k] = top
                    tot_ref[k] = jnp.sum(scaled, axis=0)
                    scaled_ref[i] = scaled.reshape(PT, QT)

    lane_block = iota((B, blocks * B), 1) // B
    active = jnp.zeros((B, blocks * B), jnp.int32)
    for k in range(blocks):
        active = jnp.where(lane_block == k, mask_s[k], active)
    active = active > 0
    score = pack_means(top_ref[...] + jnp.log(tot_ref[...]))
    logit = jnp.where(active, score / contrast_temp, very_low)
    logit_ref[...] = logit
    positive = (pos_ref[...] == iota(logit.shape, 0) + lax.axis_index("pa") * B) & active
    local_top = jnp.max(logit, axis=0, keepdims=True)
    scaled = jnp.where(active, jnp.exp(logit - local_top), 0.0)
    local_total = jnp.sum(scaled, axis=0, keepdims=True)
    local_pos = jnp.sum(jnp.where(positive, logit, 0.0), axis=0, keepdims=True)
    row = iota(logit.shape, 0)
    send = jnp.where(row == 0, local_top, jnp.where(row == 1, local_total, local_pos))
    send_ref[...] = jnp.where(row < 3, send, 0.0)


def merged(*stats):
    row = iota(stats[0].shape, 0)
    top = stats[0][:1]
    for x in stats[1:]:
        top = jnp.maximum(top, x[:1])
    total = sum(x * jnp.where(row == 1, jnp.exp(x[:1] - top), 1.0) for x in stats)
    return jnp.where(row == 0, top, total)


def grads_kernel(
    mask_hbm, pos_ref, stat0_ref, stat1_ref, stat2_ref, stat3_ref, logit_ref, tot_ref, q_ref, turn_ref, *rest
):
    blocks = tot_ref.shape[0]
    groups = blocks // GROUP
    scaled_refs, rest = rest[:groups], rest[groups:]
    loss_ref, keep_ref, give_ref, own_ref, send1_ref, send2_ref, send3_ref, *rest = rest
    mask_s, order, weight_ref, gp_ref, dsim_ref, sem = rest
    fetch = pltpu.make_async_copy(mask_hbm, mask_s, sem)
    fetch.start()
    stat = merged(stat0_ref[...], stat1_ref[...], stat2_ref[...], stat3_ref[...])
    glob_top, glob_total, glob_pos = stat[:1], stat[1:2], stat[2:3]
    loss_ref[...] = glob_top + jnp.log(glob_total) - glob_pos
    logit = logit_ref[...]
    active = logit > very_low / 2
    positive = (pos_ref[...] == iota(logit.shape, 0) + lax.axis_index("pa") * B) & active
    prob = jnp.where(active, jnp.exp(logit - glob_top) / glob_total, 0.0)
    coef = (prob - positive.astype(f32)) / (contrast_temp * LQ)
    weight_ref[...] = unpack(coef) / tot_ref[...]
    gp_ref[...] = jnp.zeros_like(gp_ref)
    fetch.wait()
    count = list_tasks(mask_s, order)
    core = lax.rem(lax.axis_index("pa"), 2)
    for group, scaled_ref in enumerate(scaled_refs):

        @pl.when(count > group * GROUP)
        def _(group=group, scaled_ref=scaled_ref):
            tasks = [order[group * GROUP + i] for i in range(GROUP)]
            for i, k in enumerate(tasks):
                dsim = (scaled_ref[i].reshape(LP, B, QT) * weight_ref[k][None]).astype(bf16)
                dsim_ref[:, i * QT : (i + 1) * QT] = dsim.reshape(PT, QT)
            queries = jnp.concatenate([block_rows(q_ref, k) for k in tasks], axis=0)
            gp_ref[...] += jnp.dot(dsim_ref[...], queries, preferred_element_type=f32)
            turned = jnp.dot(turn_ref[...], dsim_ref[...], preferred_element_type=f32)
            for i, k in enumerate(tasks):
                first, second = (turned[:, i * QT + j * D : i * QT + (j + 1) * D] for j in range(2))
                keep_ref[k] = jnp.where(core == 0, first, second)
                give_ref[k] = jnp.where(core == 0, second, first).astype(bf16)

        @pl.when(count <= group * GROUP)
        def _(group=group):
            for i in range(GROUP):
                keep_ref[order[group * GROUP + i]] = jnp.zeros(keep_ref.shape[1:], f32)
                give_ref[order[group * GROUP + i]] = jnp.zeros(give_ref.shape[1:], bf16)

    mine = lax.axis_index("pb")
    piece = PT // 4

    def rows_of(owner):
        return gp_ref[pl.ds(pl.multiple_of(owner * piece, B), piece), :]

    own_ref[...] = rows_of(mine)
    for s, send in ((1, send1_ref), (2, send2_ref), (3, send3_ref)):
        send[...] = rows_of(lax.rem(mine + s, 4)).astype(bf16)


def turn_kernel(p_ref, out_ref):
    out_ref[...] = p_ref[...].astype(f32).T.astype(bf16)


def sum_kernel(own_ref, a_ref, b_ref, c_ref, out_ref):
    total = own_ref[...] + a_ref[...].astype(f32) + b_ref[...].astype(f32) + c_ref[...].astype(f32)
    out_ref[...] = total.astype(bf16)


def both_kernel(keep_ref, got_ref, out_ref):
    out_ref[...] = (keep_ref[...] + got_ref[...].astype(f32)).astype(bf16)


def last_kernel(loss_ref, own_ref, a_ref, b_ref, c_ref, terms_ref, gp_ref, gq_ref, rows_ref):
    mine = lax.axis_index("pb")
    piece = PT // 4
    for s, ref in ((0, own_ref), (1, a_ref), (2, b_ref), (3, c_ref)):
        owner = lax.rem(mine + 4 - s, 4)
        gp_ref[pl.ds(pl.multiple_of(owner * piece, B), piece), :] = ref[...].astype(f32)
    total = terms_ref[0].astype(f32)
    for i in range(1, terms_ref.shape[0]):
        total += terms_ref[i].astype(f32)
    gq_ref[...] = total.T
    count, own = loss_ref.shape[1], rows_ref.shape[1]
    pick = iota((count, own), 0) == iota((count, own), 1) + own * lax.axis_index("pa")
    rows_ref[...] = exact_dot(loss_ref[...], pick.astype(f32))


def in_hbm(x):
    return pltpu.with_memory_space_constraint(x, pltpu.HBM)


def call(kernel, out, specs, scratch=(), vmem=16 << 20, flops=0, nbytes=0):
    return pl.pallas_call(
        kernel,
        out_shape=out,
        in_specs=list(specs),
        out_specs=jax.tree.map(lambda _: VMEM, out),
        scratch_shapes=list(scratch),
        compiler_params=pltpu.CompilerParams(vmem_limit_bytes=vmem),
        cost_estimate=pl.CostEstimate(flops=flops, bytes_accessed=nbytes, transcendentals=0),
    )


def turn(x, s):
    return lax.ppermute(x, "pb", [(i, (i + s) % 4) for i in range(4)])


def turn_digit(x, s, unit):
    def to(i):
        return i + unit * ((i // unit + s) % 4 - i // unit % 4)

    return lax.ppermute(x, "pa", [(i, to(i)) for i in range(lax.axis_size("pa"))])


def on_device(queries, passages, pair_mask, positive):
    rows = queries.shape[0]
    blocks = rows // B
    groups = blocks // GROUP
    peers = lax.axis_size("pa")
    own_rows = rows // peers
    shape = jax.ShapeDtypeStruct
    flat_q = queries.reshape(rows * LQ, D)
    flat_p = jnp.swapaxes(passages, 0, 1).reshape(PT, D)
    mask = pair_mask.reshape(blocks)
    pos = positive.reshape(1, rows)
    ints = pltpu.SMEM((blocks,), jnp.int32)
    mask, flat_q, flat_p = (in_hbm(x) for x in (mask, flat_q, flat_p))
    wide = shape((blocks, B, QT), f32)
    packed = shape((B, rows), f32)
    send, logit, tot, near_q, near_p, *scaled = call(
        scores_kernel,
        (
            packed,
            packed,
            wide,
            shape((rows * LQ, D), bf16),
            shape((PT, D), bf16),
            *(shape((GROUP, PT, QT), f32),) * groups,
        ),
        (ANY,) * 4,
        [
            ints,
            pltpu.VMEM((1, rows), jnp.int32),
            ints,
            pltpu.VMEM((blocks, B, QT), f32),
            pltpu.VMEM((PT, QT), f32),
            pltpu.SemaphoreType.DMA((4,)),
        ],
        flops=2_000_000_000,
        nbytes=3_000_000,
    )(mask, in_hbm(pos), flat_q, flat_p)
    stat = merged(send, lax.ppermute(send, "pa", [(i, i ^ 1) for i in range(peers)]))
    stat = merged(stat, *(turn_digit(stat, s, 2) for s in (1, 2, 3)))
    stats = (stat, *(turn_digit(stat, s, 8) for s in (3, 2, 1)))
    turned_p = call(turn_kernel, shape((D, PT), bf16), (VMEM,), nbytes=100_000)(near_p)
    piece = shape((PT // 4, D), bf16)
    half = shape((blocks, D, own_rows * LQ), bf16)
    loss, keep, give, own, send1, send2, send3 = call(
        grads_kernel,
        (
            shape((1, rows), f32),
            shape((blocks, D, own_rows * LQ), f32),
            half,
            shape((PT // 4, D), f32),
            piece,
            piece,
            piece,
        ),
        (ANY,) + (VMEM,) * (9 + groups),
        [
            ints,
            ints,
            pltpu.VMEM((blocks, B, QT), f32),
            pltpu.VMEM((PT, D), f32),
            pltpu.VMEM((PT, GROUP * QT), bf16),
            pltpu.SemaphoreType.DMA,
        ],
        flops=5_000_000_000,
        nbytes=5_000_000,
    )(mask, pos, *stats, logit, tot, near_q, turned_p, *scaled)
    sends = {1: send1, 2: send2, 3: send3}
    got = [turn(sends[s], s) for s in (1, 2, 3)]
    got_half = lax.ppermute(give, "pa", [(i, i ^ 1) for i in range(peers)])
    both = call(both_kernel, half, (VMEM,) * 2, flops=10_000_000_000)(keep, got_half)
    same_core = [list(range(core, peers, 2)) for core in range(2)]
    gq_terms = lax.all_to_all(both, "pa", 0, 0, axis_index_groups=same_core, tiled=True)
    mine = call(sum_kernel, piece, (VMEM,) * 4, flops=30_000_000_000)(own, *got)
    others = [turn(mine, s) for s in (1, 2, 3)]
    flat, grad_q, loss_rows = call(
        last_kernel,
        (shape((PT, D), f32), shape((own_rows * LQ, D), f32), shape((1, own_rows), f32)),
        (VMEM,) * 6,
        nbytes=2_000_000,
    )(loss, mine, *others, gq_terms)
    grad_p = jnp.swapaxes(flat.reshape(LP, B, D), 0, 1)
    return loss_rows.reshape(own_rows), grad_q.reshape(own_rows, LQ, D), grad_p


def solution(mesh):
    placed = (P("pb", None, None), P("pa", None, None), P("pb", "pa"), P("pb"))
    return jax.shard_map(
        on_device,
        mesh=mesh,
        in_specs=placed,
        out_specs=(P(("pb", "pa")), P(("pb", "pa"), None, None), P("pa", None, None)),
        check_vma=False,
    )
```

```python
import jax
import jax.numpy as jnp
from jax import lax
from jax.experimental import pallas as pl
from jax.experimental.pallas import tpu as pltpu
from jax.sharding import PartitionSpec as P

very_low = -1e30
contrast_temp = 0.05
safe_low, safe_high = 1e-12, 1e12
f32, bf16 = jnp.float32, jnp.bfloat16
VMEM = pl.BlockSpec(memory_space=pltpu.VMEM)
ANY = pl.BlockSpec(memory_space=pl.ANY)
B, LQ, LP, D = 8, 32, 180, 128
QT = B * LQ
PT = B * LP
GROUP = 4
turned_dims = (((1,), (1,)), ((), ()))


def iota(shape, dim):
    return lax.broadcasted_iota(jnp.int32, shape, dim)


def exact_dot(a, b):
    return jnp.dot(a, b, precision=lax.Precision.HIGHEST, preferred_element_type=f32)


def own_lanes(blocks):
    return iota((blocks, B, blocks * B), 2) // B == iota((blocks, B, blocks * B), 0)


def pack_means(wide):
    blocks = wide.shape[0]
    count = blocks * B
    pick = (iota((QT, count), 0) // LQ == iota((QT, count), 1) % B).astype(f32)
    sums = exact_dot(wide.reshape(count, QT), pick).reshape(blocks, B, count)
    return jnp.sum(jnp.where(own_lanes(blocks), sums, 0.0), axis=0) / LQ


def unpack(packed):
    count = packed.shape[1]
    blocks = count // B
    pick = (iota((count, QT), 0) % B == iota((count, QT), 1) // LQ).astype(f32)
    spread = jnp.where(own_lanes(blocks), packed[None], 0.0).reshape(count, count)
    return exact_dot(spread, pick).reshape(blocks, B, QT)


def list_tasks(mask_s, order):
    blocks = mask_s.shape[0]
    count = jnp.int32(0)
    for wanted in (True, False):
        for k in range(blocks):
            here = (mask_s[k] > 0) == wanted

            @pl.when(here)
            def _(k=k, count=count):
                order[count] = k

            count = count + here.astype(jnp.int32)
        if wanted:
            active = count
    return active


def block_rows(q_ref, k):
    return q_ref[pl.ds(pl.multiple_of(k * QT, QT), QT), :]


def fetch_all(pairs, sems):
    fetches = [pltpu.make_async_copy(src, dst, sems.at[i]) for i, (src, dst) in enumerate(pairs)]
    for fetch in fetches:
        fetch.start()
    return [fetch.wait for fetch in fetches]


def task_sim(p_ref, q_ref, k):
    return lax.dot_general(p_ref[...], block_rows(q_ref, k), turned_dims, preferred_element_type=f32)


def scores_kernel(mask_hbm, pos_hbm, q_hbm, p_hbm, send_ref, logit_ref, tot_ref, q_ref, p_ref, *rest):
    blocks = tot_ref.shape[0]
    groups = blocks // GROUP
    scaled_refs, (mask_s, pos_ref, order, top_ref, sim_ref, sems) = rest[:groups], rest[groups:]
    pairs = ((mask_hbm, mask_s), (pos_hbm, pos_ref), (p_hbm, p_ref), (q_hbm, q_ref))
    mask_wait, pos_wait, p_wait, q_wait = fetch_all(pairs, sems)
    top_ref[...] = jnp.zeros_like(top_ref)
    tot_ref[...] = jnp.ones_like(tot_ref)
    mask_wait()
    count = list_tasks(mask_s, order)
    pos_wait()
    p_wait()
    q_wait()
    for group, scaled_ref in enumerate(scaled_refs):

        @pl.when(count > group * GROUP)
        def _(group=group, scaled_ref=scaled_ref):
            for i in range(GROUP):
                k = order[group * GROUP + i]
                scaled = jnp.exp(task_sim(p_ref, q_ref, k))
                scaled_ref[i] = scaled
                tot_ref[k] = jnp.sum(scaled.reshape(LP, B, QT), axis=0)

    safe = (jnp.min(tot_ref[...]) > safe_low) & (jnp.max(tot_ref[...]) < safe_high)

    @pl.when(jnp.logical_not(safe))
    def _():
        for group, scaled_ref in enumerate(scaled_refs):

            @pl.when(count > group * GROUP)
            def _(group=group, scaled_ref=scaled_ref):
                @pl.loop(0, GROUP)
                def _(i):
                    k = order[group * GROUP + i]
                    sim_ref[...] = task_sim(p_ref, q_ref, k)
                    sim = sim_ref[...].reshape(LP, B, QT)
                    top = jnp.max(sim, axis=0)
                    scaled = jnp.exp(sim - top[None])
                    top_ref[k] = top
                    tot_ref[k] = jnp.sum(scaled, axis=0)
                    scaled_ref[i] = scaled.reshape(PT, QT)

    lane_block = iota((B, blocks * B), 1) // B
    active = jnp.zeros((B, blocks * B), jnp.int32)
    for k in range(blocks):
        active = jnp.where(lane_block == k, mask_s[k], active)
    active = active > 0
    score = pack_means(top_ref[...] + jnp.log(tot_ref[...]))
    logit = jnp.where(active, score / contrast_temp, very_low)
    logit_ref[...] = logit
    positive = (pos_ref[...] == iota(logit.shape, 0) + lax.axis_index("pa") * B) & active
    local_top = jnp.max(logit, axis=0, keepdims=True)
    scaled = jnp.where(active, jnp.exp(logit - local_top), 0.0)
    local_total = jnp.sum(scaled, axis=0, keepdims=True)
    local_pos = jnp.sum(jnp.where(positive, logit, 0.0), axis=0, keepdims=True)
    row = iota(logit.shape, 0)
    send = jnp.where(row == 0, local_top, jnp.where(row == 1, local_total, local_pos))
    send_ref[...] = jnp.where(row < 3, send, 0.0)


def merged(*stats):
    row = iota(stats[0].shape, 0)
    top = stats[0][:1]
    for x in stats[1:]:
        top = jnp.maximum(top, x[:1])
    total = sum(x * jnp.where(row == 1, jnp.exp(x[:1] - top), 1.0) for x in stats)
    return jnp.where(row == 0, top, total)


def grads_kernel(
    mask_hbm, pos_ref, stat0_ref, stat1_ref, stat2_ref, stat3_ref, logit_ref, tot_ref, q_ref, turn_ref, *rest
):
    blocks = tot_ref.shape[0]
    groups = blocks // GROUP
    scaled_refs, rest = rest[:groups], rest[groups:]
    loss_ref, keep_ref, give_ref, own_ref, send1_ref, send2_ref, send3_ref, *rest = rest
    mask_s, order, weight_ref, gp_ref, dsim_ref, sem = rest
    fetch = pltpu.make_async_copy(mask_hbm, mask_s, sem)
    fetch.start()
    stat = merged(stat0_ref[...], stat1_ref[...], stat2_ref[...], stat3_ref[...])
    glob_top, glob_total, glob_pos = stat[:1], stat[1:2], stat[2:3]
    loss_ref[...] = glob_top + jnp.log(glob_total) - glob_pos
    logit = logit_ref[...]
    active = logit > very_low / 2
    positive = (pos_ref[...] == iota(logit.shape, 0) + lax.axis_index("pa") * B) & active
    prob = jnp.where(active, jnp.exp(logit - glob_top) / glob_total, 0.0)
    coef = (prob - positive.astype(f32)) / (contrast_temp * LQ)
    weight_ref[...] = unpack(coef) / tot_ref[...]
    gp_ref[...] = jnp.zeros_like(gp_ref)
    fetch.wait()
    count = list_tasks(mask_s, order)
    core = lax.rem(lax.axis_index("pa"), 2)
    for group, scaled_ref in enumerate(scaled_refs):

        @pl.when(count > group * GROUP)
        def _(group=group, scaled_ref=scaled_ref):
            tasks = [order[group * GROUP + i] for i in range(GROUP)]
            for i, k in enumerate(tasks):
                dsim = (scaled_ref[i].reshape(LP, B, QT) * weight_ref[k][None]).astype(bf16)
                dsim_ref[:, i * QT : (i + 1) * QT] = dsim.reshape(PT, QT)
            queries = jnp.concatenate([block_rows(q_ref, k) for k in tasks], axis=0)
            gp_ref[...] += jnp.dot(dsim_ref[...], queries, preferred_element_type=f32)
            turned = jnp.dot(turn_ref[...], dsim_ref[...], preferred_element_type=f32)
            for i, k in enumerate(tasks):
                first, second = (turned[:, i * QT + j * D : i * QT + (j + 1) * D] for j in range(2))
                keep_ref[k] = jnp.where(core == 0, first, second)
                give_ref[k] = jnp.where(core == 0, second, first)

        @pl.when(count <= group * GROUP)
        def _(group=group):
            for i in range(GROUP):
                keep_ref[order[group * GROUP + i]] = jnp.zeros(keep_ref.shape[1:], f32)
                give_ref[order[group * GROUP + i]] = jnp.zeros(give_ref.shape[1:], f32)

    mine = lax.axis_index("pb")
    piece = PT // 4

    def rows_of(owner):
        return gp_ref[pl.ds(pl.multiple_of(owner * piece, B), piece), :]

    own_ref[...] = rows_of(mine)
    for s, send in ((1, send1_ref), (2, send2_ref), (3, send3_ref)):
        send[...] = rows_of(lax.rem(mine + s, 4)).astype(bf16)


def turn_kernel(p_ref, out_ref):
    out_ref[...] = p_ref[...].astype(f32).T.astype(bf16)


def sum_kernel(own_ref, a_ref, b_ref, c_ref, out_ref):
    total = own_ref[...] + a_ref[...].astype(f32) + b_ref[...].astype(f32) + c_ref[...].astype(f32)
    out_ref[...] = total.astype(bf16)


def both_kernel(keep_ref, got_ref, out_ref):
    out_ref[...] = (keep_ref[...] + got_ref[...]).astype(bf16)


def place_kernel(loss_ref, own_ref, a_ref, b_ref, c_ref, gp_ref, rows_ref):
    mine = lax.axis_index("pb")
    piece = PT // 4
    for s, ref in ((0, own_ref), (1, a_ref), (2, b_ref), (3, c_ref)):
        owner = lax.rem(mine + 4 - s, 4)
        gp_ref[pl.ds(pl.multiple_of(owner * piece, B), piece), :] = ref[...].astype(f32)
    count, own = loss_ref.shape[1], rows_ref.shape[1]
    pick = iota((count, own), 0) == iota((count, own), 1) + own * lax.axis_index("pa")
    rows_ref[...] = exact_dot(loss_ref[...], pick.astype(f32))


def rows_kernel(terms_ref, gq_ref):
    total = terms_ref[0].astype(f32)
    for i in range(1, terms_ref.shape[0]):
        total += terms_ref[i].astype(f32)
    gq_ref[...] = total.T


def in_hbm(x):
    return pltpu.with_memory_space_constraint(x, pltpu.HBM)


def call(kernel, out, specs, scratch=(), vmem=16 << 20, flops=0, nbytes=0):
    return pl.pallas_call(
        kernel,
        out_shape=out,
        in_specs=list(specs),
        out_specs=jax.tree.map(lambda _: VMEM, out),
        scratch_shapes=list(scratch),
        compiler_params=pltpu.CompilerParams(vmem_limit_bytes=vmem),
        cost_estimate=pl.CostEstimate(flops=flops, bytes_accessed=nbytes, transcendentals=0),
    )


def turn(x, s):
    return lax.ppermute(x, "pb", [(i, (i + s) % 4) for i in range(4)])


def turn_digit(x, s, unit):
    def to(i):
        return i + unit * ((i // unit + s) % 4 - i // unit % 4)

    return lax.ppermute(x, "pa", [(i, to(i)) for i in range(lax.axis_size("pa"))])


def on_device(queries, passages, pair_mask, positive):
    rows = queries.shape[0]
    blocks = rows // B
    groups = blocks // GROUP
    peers = lax.axis_size("pa")
    own_rows = rows // peers
    shape = jax.ShapeDtypeStruct
    flat_q = queries.reshape(rows * LQ, D)
    flat_p = jnp.swapaxes(passages, 0, 1).reshape(PT, D)
    mask = pair_mask.reshape(blocks)
    pos = positive.reshape(1, rows)
    ints = pltpu.SMEM((blocks,), jnp.int32)
    mask, flat_q, flat_p = (in_hbm(x) for x in (mask, flat_q, flat_p))
    wide = shape((blocks, B, QT), f32)
    packed = shape((B, rows), f32)
    send, logit, tot, near_q, near_p, *scaled = call(
        scores_kernel,
        (
            packed,
            packed,
            wide,
            shape((rows * LQ, D), bf16),
            shape((PT, D), bf16),
            *(shape((GROUP, PT, QT), f32),) * groups,
        ),
        (ANY,) * 4,
        [
            ints,
            pltpu.VMEM((1, rows), jnp.int32),
            ints,
            pltpu.VMEM((blocks, B, QT), f32),
            pltpu.VMEM((PT, QT), f32),
            pltpu.SemaphoreType.DMA((4,)),
        ],
        flops=2_000_000_000,
        nbytes=3_000_000,
    )(mask, in_hbm(pos), flat_q, flat_p)
    stat = merged(send, lax.ppermute(send, "pa", [(i, i ^ 1) for i in range(peers)]))
    stat = merged(stat, *(turn_digit(stat, s, 2) for s in (1, 2, 3)))
    stats = (stat, *(turn_digit(stat, s, 8) for s in (3, 2, 1)))
    turned_p = call(turn_kernel, shape((D, PT), bf16), (VMEM,), nbytes=100_000)(near_p)
    piece = shape((PT // 4, D), bf16)
    half = shape((blocks, D, own_rows * LQ), f32)
    loss, keep, give, own, send1, send2, send3 = call(
        grads_kernel,
        (
            shape((1, rows), f32),
            half,
            half,
            shape((PT // 4, D), f32),
            piece,
            piece,
            piece,
        ),
        (ANY,) + (VMEM,) * (9 + groups),
        [
            ints,
            ints,
            pltpu.VMEM((blocks, B, QT), f32),
            pltpu.VMEM((PT, D), f32),
            pltpu.VMEM((PT, GROUP * QT), bf16),
            pltpu.SemaphoreType.DMA,
        ],
        flops=5_000_000_000,
        nbytes=5_000_000,
    )(mask, pos, *stats, logit, tot, near_q, turned_p, *scaled)
    sends = {1: send1, 2: send2, 3: send3}
    got = [turn(sends[s], s) for s in (3, 2, 1)]
    got_half = lax.ppermute(give, "pa", [(i, i ^ 1) for i in range(peers)])
    both = call(both_kernel, shape(half.shape, bf16), (VMEM,) * 2, flops=10_000_000_000)(keep, got_half)
    same_core = [list(range(core, peers, 2)) for core in range(2)]
    gq_terms = lax.all_to_all(both, "pa", 0, 0, axis_index_groups=same_core, tiled=True)
    mine = call(sum_kernel, piece, (VMEM,) * 4, flops=30_000_000_000)(own, *got)
    others = [turn(mine, s) for s in (1, 2, 3)]
    flat, loss_rows = call(
        place_kernel, (shape((PT, D), f32), shape((1, own_rows), f32)), (VMEM,) * 5, nbytes=1_000_000
    )(loss, mine, *others)
    grad_q = call(rows_kernel, shape((own_rows * LQ, D), f32), (VMEM,), nbytes=1_000_000)(gq_terms)
    grad_p = jnp.swapaxes(flat.reshape(LP, B, D), 0, 1)
    return loss_rows.reshape(own_rows), grad_q.reshape(own_rows, LQ, D), grad_p


def solution(mesh):
    placed = (P("pb", None, None), P("pa", None, None), P("pb", "pa"), P("pb"))
    return jax.shard_map(
        on_device,
        mesh=mesh,
        in_specs=placed,
        out_specs=(P(("pb", "pa")), P(("pb", "pa"), None, None), P("pa", None, None)),
        check_vma=False,
    )
```

```python
import jax
import jax.numpy as jnp
from jax import lax
from jax.experimental import pallas as pl
from jax.experimental.pallas import tpu as pltpu
from jax.sharding import PartitionSpec as P

very_low = -1e30
contrast_temp = 0.05
safe_low, safe_high = 1e-12, 1e12
f32, bf16 = jnp.float32, jnp.bfloat16
VMEM = pl.BlockSpec(memory_space=pltpu.VMEM)
ANY = pl.BlockSpec(memory_space=pl.ANY)
B, LQ, LP, D = 8, 32, 180, 128
QT = B * LQ
PT = B * LP
GROUP = 4
turned_dims = (((1,), (1,)), ((), ()))


def iota(shape, dim):
    return lax.broadcasted_iota(jnp.int32, shape, dim)


def exact_dot(a, b):
    return jnp.dot(a, b, precision=lax.Precision.HIGHEST, preferred_element_type=f32)


def own_lanes(blocks):
    return iota((blocks, B, blocks * B), 2) // B == iota((blocks, B, blocks * B), 0)


def pack_means(wide):
    blocks = wide.shape[0]
    count = blocks * B
    pick = (iota((QT, count), 0) // LQ == iota((QT, count), 1) % B).astype(f32)
    sums = exact_dot(wide.reshape(count, QT), pick).reshape(blocks, B, count)
    return jnp.sum(jnp.where(own_lanes(blocks), sums, 0.0), axis=0) / LQ


def unpack(packed):
    count = packed.shape[1]
    blocks = count // B
    pick = (iota((count, QT), 0) % B == iota((count, QT), 1) // LQ).astype(f32)
    spread = jnp.where(own_lanes(blocks), packed[None], 0.0).reshape(count, count)
    return exact_dot(spread, pick).reshape(blocks, B, QT)


def list_tasks(mask_s, order):
    blocks = mask_s.shape[0]
    count = jnp.int32(0)
    for wanted in (True, False):
        for k in range(blocks):
            here = (mask_s[k] > 0) == wanted

            @pl.when(here)
            def _(k=k, count=count):
                order[count] = k

            count = count + here.astype(jnp.int32)
        if wanted:
            active = count
    return active


def block_rows(q_ref, k):
    return q_ref[pl.ds(pl.multiple_of(k * QT, QT), QT), :]


def fetch_all(pairs, sems):
    fetches = [pltpu.make_async_copy(src, dst, sems.at[i]) for i, (src, dst) in enumerate(pairs)]
    for fetch in fetches:
        fetch.start()
    return [fetch.wait for fetch in fetches]


def task_sim(p_ref, q_ref, k):
    return lax.dot_general(p_ref[...], block_rows(q_ref, k), turned_dims, preferred_element_type=f32)


def scores_kernel(mask_hbm, pos_hbm, q_hbm, p_hbm, send_ref, logit_ref, tot_ref, q_ref, turn_ref, *rest):
    blocks = tot_ref.shape[0]
    groups = blocks // GROUP
    scaled_refs, (mask_s, pos_ref, p_ref, order, top_ref, sim_ref, sems) = rest[:groups], rest[groups:]
    pairs = ((mask_hbm, mask_s), (pos_hbm, pos_ref), (p_hbm, p_ref), (q_hbm, q_ref))
    mask_wait, pos_wait, p_wait, q_wait = fetch_all(pairs, sems)
    top_ref[...] = jnp.zeros_like(top_ref)
    tot_ref[...] = jnp.ones_like(tot_ref)
    mask_wait()
    count = list_tasks(mask_s, order)
    pos_wait()
    p_wait()
    turn_ref[...] = p_ref[...].astype(f32).T.astype(bf16)
    q_wait()
    for group, scaled_ref in enumerate(scaled_refs):

        @pl.when(count > group * GROUP)
        def _(group=group, scaled_ref=scaled_ref):
            for i in range(GROUP):
                k = order[group * GROUP + i]
                scaled = jnp.exp(task_sim(p_ref, q_ref, k))
                scaled_ref[i] = scaled
                tot_ref[k] = jnp.sum(scaled.reshape(LP, B, QT), axis=0)

    safe = (jnp.min(tot_ref[...]) > safe_low) & (jnp.max(tot_ref[...]) < safe_high)

    @pl.when(jnp.logical_not(safe))
    def _():
        for group, scaled_ref in enumerate(scaled_refs):

            @pl.when(count > group * GROUP)
            def _(group=group, scaled_ref=scaled_ref):
                @pl.loop(0, GROUP)
                def _(i):
                    k = order[group * GROUP + i]
                    sim_ref[...] = task_sim(p_ref, q_ref, k)
                    sim = sim_ref[...].reshape(LP, B, QT)
                    top = jnp.max(sim, axis=0)
                    scaled = jnp.exp(sim - top[None])
                    top_ref[k] = top
                    tot_ref[k] = jnp.sum(scaled, axis=0)
                    scaled_ref[i] = scaled.reshape(PT, QT)

    lane_block = iota((B, blocks * B), 1) // B
    active = jnp.zeros((B, blocks * B), jnp.int32)
    for k in range(blocks):
        active = jnp.where(lane_block == k, mask_s[k], active)
    active = active > 0
    score = pack_means(top_ref[...] + jnp.log(tot_ref[...]))
    logit = jnp.where(active, score / contrast_temp, very_low)
    logit_ref[...] = logit
    positive = (pos_ref[...] == iota(logit.shape, 0) + lax.axis_index("pa") * B) & active
    local_top = jnp.max(logit, axis=0, keepdims=True)
    scaled = jnp.where(active, jnp.exp(logit - local_top), 0.0)
    local_total = jnp.sum(scaled, axis=0, keepdims=True)
    local_pos = jnp.sum(jnp.where(positive, logit, 0.0), axis=0, keepdims=True)
    row = iota(logit.shape, 0)
    send = jnp.where(row == 0, local_top, jnp.where(row == 1, local_total, local_pos))
    send_ref[...] = jnp.broadcast_to(jnp.where(row < 3, send, 0.0)[None], send_ref.shape)


def grads_kernel(
    mask_hbm, pos_ref, stat_ref, logit_ref, tot_ref, q_ref, turn_ref, *rest
):
    blocks = tot_ref.shape[0]
    groups = blocks // GROUP
    scaled_refs, rest = rest[:groups], rest[groups:]
    loss_ref, keep_ref, give_ref, own_ref, send1_ref, send2_ref, send3_ref, *rest = rest
    mask_s, order, weight_ref, gp_ref, dsim_ref, sem = rest
    fetch = pltpu.make_async_copy(mask_hbm, mask_s, sem)
    fetch.start()
    stat = stat_ref[...]
    top = jnp.max(stat, axis=0)[:1]
    row = iota(stat.shape, 1)
    sums = jnp.sum(stat * jnp.where(row == 1, jnp.exp(stat[:, :1] - top[None]), 1.0), axis=0)
    glob_top, glob_total, glob_pos = top, sums[1:2], sums[2:3]
    loss_ref[...] = glob_top + jnp.log(glob_total) - glob_pos
    logit = logit_ref[...]
    active = logit > very_low / 2
    positive = (pos_ref[...] == iota(logit.shape, 0) + lax.axis_index("pa") * B) & active
    prob = jnp.where(active, jnp.exp(logit - glob_top) / glob_total, 0.0)
    coef = (prob - positive.astype(f32)) / (contrast_temp * LQ)
    weight_ref[...] = unpack(coef) / tot_ref[...]
    gp_ref[...] = jnp.zeros_like(gp_ref)
    fetch.wait()
    count = list_tasks(mask_s, order)
    core = lax.rem(lax.axis_index("pa"), 2)
    for group, scaled_ref in enumerate(scaled_refs):

        @pl.when(count > group * GROUP)
        def _(group=group, scaled_ref=scaled_ref):
            tasks = [order[group * GROUP + i] for i in range(GROUP)]
            for i, k in enumerate(tasks):
                dsim = (scaled_ref[i].reshape(LP, B, QT) * weight_ref[k][None]).astype(bf16)
                dsim_ref[:, i * QT : (i + 1) * QT] = dsim.reshape(PT, QT)
            queries = jnp.concatenate([block_rows(q_ref, k) for k in tasks], axis=0)
            gp_ref[...] += jnp.dot(dsim_ref[...], queries, preferred_element_type=f32)
            turned = jnp.dot(turn_ref[...], dsim_ref[...], preferred_element_type=f32)
            for i, k in enumerate(tasks):
                first, second = (turned[:, i * QT + j * D : i * QT + (j + 1) * D] for j in range(2))
                keep_ref[k] = jnp.where(core == 0, first, second)
                give_ref[k] = jnp.where(core == 0, second, first)

        @pl.when(count <= group * GROUP)
        def _(group=group):
            for i in range(GROUP):
                keep_ref[order[group * GROUP + i]] = jnp.zeros(keep_ref.shape[1:], f32)
                give_ref[order[group * GROUP + i]] = jnp.zeros(give_ref.shape[1:], f32)

    mine = lax.axis_index("pb")
    piece = PT // 4

    def rows_of(owner):
        return gp_ref[pl.ds(pl.multiple_of(owner * piece, B), piece), :]

    own_ref[...] = rows_of(mine)
    for s, send in ((1, send1_ref), (2, send2_ref), (3, send3_ref)):
        send[...] = rows_of(lax.rem(mine + s, 4)).astype(bf16)


def sum_kernel(own_ref, a_ref, b_ref, c_ref, out_ref):
    total = own_ref[...] + a_ref[...].astype(f32) + b_ref[...].astype(f32) + c_ref[...].astype(f32)
    out_ref[...] = total.astype(bf16)


def both_kernel(keep_ref, got_ref, out_ref):
    out_ref[...] = (keep_ref[...] + got_ref[...]).astype(bf16)


def place_kernel(loss_ref, own_ref, a_ref, b_ref, c_ref, gp_ref, rows_ref):
    mine = lax.axis_index("pb")
    piece = PT // 4
    for s, ref in ((0, own_ref), (1, a_ref), (2, b_ref), (3, c_ref)):
        owner = lax.rem(mine + 4 - s, 4)
        gp_ref[pl.ds(pl.multiple_of(owner * piece, B), piece), :] = ref[...].astype(f32)
    count, own = loss_ref.shape[1], rows_ref.shape[1]
    pick = iota((count, own), 0) == iota((count, own), 1) + own * lax.axis_index("pa")
    rows_ref[...] = exact_dot(loss_ref[...], pick.astype(f32))


def rows_kernel(terms_ref, gq_ref):
    total = terms_ref[0].astype(f32)
    for i in range(1, terms_ref.shape[0]):
        total += terms_ref[i].astype(f32)
    gq_ref[...] = total.T


def in_hbm(x):
    return pltpu.with_memory_space_constraint(x, pltpu.HBM)


def call(kernel, out, specs, scratch=(), vmem=16 << 20, flops=0, nbytes=0):
    return pl.pallas_call(
        kernel,
        out_shape=out,
        in_specs=list(specs),
        out_specs=jax.tree.map(lambda _: VMEM, out),
        scratch_shapes=list(scratch),
        compiler_params=pltpu.CompilerParams(vmem_limit_bytes=vmem),
        cost_estimate=pl.CostEstimate(flops=flops, bytes_accessed=nbytes, transcendentals=0),
    )


def turn(x, s):
    return lax.ppermute(x, "pb", [(i, (i + s) % 4) for i in range(4)])


def on_device(queries, passages, pair_mask, positive):
    rows = queries.shape[0]
    blocks = rows // B
    groups = blocks // GROUP
    peers = lax.axis_size("pa")
    own_rows = rows // peers
    shape = jax.ShapeDtypeStruct
    flat_q = queries.reshape(rows * LQ, D)
    flat_p = jnp.swapaxes(passages, 0, 1).reshape(PT, D)
    mask = pair_mask.reshape(blocks)
    pos = positive.reshape(1, rows)
    ints = pltpu.SMEM((blocks,), jnp.int32)
    mask, flat_q, flat_p = (in_hbm(x) for x in (mask, flat_q, flat_p))
    wide = shape((blocks, B, QT), f32)
    packed = shape((B, rows), f32)
    send, logit, tot, near_q, turned_p, *scaled = call(
        scores_kernel,
        (
            shape((peers, B, rows), f32),
            packed,
            wide,
            shape((rows * LQ, D), bf16),
            shape((D, PT), bf16),
            *(shape((GROUP, PT, QT), f32),) * groups,
        ),
        (ANY,) * 4,
        [
            ints,
            pltpu.VMEM((1, rows), jnp.int32),
            pltpu.VMEM((PT, D), bf16),
            ints,
            pltpu.VMEM((blocks, B, QT), f32),
            pltpu.VMEM((PT, QT), f32),
            pltpu.SemaphoreType.DMA((4,)),
        ],
        flops=2_000_000_000,
        nbytes=3_000_000,
    )(mask, in_hbm(pos), flat_q, flat_p)
    stats = lax.all_to_all(send, "pa", 0, 0, tiled=True)
    piece = shape((PT // 4, D), bf16)
    half = shape((blocks, D, own_rows * LQ), f32)
    loss, keep, give, own, send1, send2, send3 = call(
        grads_kernel,
        (
            shape((1, rows), f32),
            half,
            half,
            shape((PT // 4, D), f32),
            piece,
            piece,
            piece,
        ),
        (ANY,) + (VMEM,) * (6 + groups),
        [
            ints,
            ints,
            pltpu.VMEM((blocks, B, QT), f32),
            pltpu.VMEM((PT, D), f32),
            pltpu.VMEM((PT, GROUP * QT), bf16),
            pltpu.SemaphoreType.DMA,
        ],
        flops=5_000_000_000,
        nbytes=5_000_000,
    )(mask, pos, stats, logit, tot, near_q, turned_p, *scaled)
    sends = {1: send1, 2: send2, 3: send3}
    got = [turn(sends[s], s) for s in (3, 2, 1)]
    got_half = lax.ppermute(give, "pa", [(i, i ^ 1) for i in range(peers)])
    both = call(both_kernel, shape(half.shape, bf16), (VMEM,) * 2, flops=10_000_000_000)(keep, got_half)
    same_core = [list(range(core, peers, 2)) for core in range(2)]
    gq_terms = lax.all_to_all(both, "pa", 0, 0, axis_index_groups=same_core, tiled=True)
    mine = call(sum_kernel, piece, (VMEM,) * 4, flops=30_000_000_000)(own, *got)
    others = [turn(mine, s) for s in (1, 2, 3)]
    flat, loss_rows = call(
        place_kernel, (shape((PT, D), f32), shape((1, own_rows), f32)), (VMEM,) * 5, nbytes=1_000_000
    )(loss, mine, *others)
    grad_q = call(rows_kernel, shape((own_rows * LQ, D), f32), (VMEM,), nbytes=1_000_000)(gq_terms)
    grad_p = jnp.swapaxes(flat.reshape(LP, B, D), 0, 1)
    return loss_rows.reshape(own_rows), grad_q.reshape(own_rows, LQ, D), grad_p


def solution(mesh):
    placed = (P("pb", None, None), P("pa", None, None), P("pb", "pa"), P("pb"))
    return jax.shard_map(
        on_device,
        mesh=mesh,
        in_specs=placed,
        out_specs=(P(("pb", "pa")), P(("pb", "pa"), None, None), P("pa", None, None)),
        check_vma=False,
    )
```

```python
import jax
import jax.numpy as jnp
from jax import lax
from jax.experimental import pallas as pl
from jax.experimental.pallas import tpu as pltpu
from jax.sharding import PartitionSpec as P

very_low = -1e30
contrast_temp = 0.05
safe_low, safe_high = 1e-12, 1e12
f32, bf16 = jnp.float32, jnp.bfloat16
VMEM = pl.BlockSpec(memory_space=pltpu.VMEM)
ANY = pl.BlockSpec(memory_space=pl.ANY)
B, LQ, LP, D = 8, 32, 180, 128
QT = B * LQ
PT = B * LP
GROUP = 4
turned_dims = (((1,), (1,)), ((), ()))


def iota(shape, dim):
    return lax.broadcasted_iota(jnp.int32, shape, dim)


def exact_dot(a, b):
    return jnp.dot(a, b, precision=lax.Precision.HIGHEST, preferred_element_type=f32)


def own_lanes(blocks):
    return iota((blocks, B, blocks * B), 2) // B == iota((blocks, B, blocks * B), 0)


def pack_means(wide):
    blocks = wide.shape[0]
    count = blocks * B
    pick = (iota((QT, count), 0) // LQ == iota((QT, count), 1) % B).astype(f32)
    sums = exact_dot(wide.reshape(count, QT), pick).reshape(blocks, B, count)
    return jnp.sum(jnp.where(own_lanes(blocks), sums, 0.0), axis=0) / LQ


def unpack(packed):
    count = packed.shape[1]
    blocks = count // B
    pick = (iota((count, QT), 0) % B == iota((count, QT), 1) // LQ).astype(f32)
    spread = jnp.where(own_lanes(blocks), packed[None], 0.0).reshape(count, count)
    return exact_dot(spread, pick).reshape(blocks, B, QT)


def list_tasks(mask_s, order):
    blocks = mask_s.shape[0]
    count = jnp.int32(0)
    for wanted in (True, False):
        for k in range(blocks):
            here = (mask_s[k] > 0) == wanted

            @pl.when(here)
            def _(k=k, count=count):
                order[count] = k

            count = count + here.astype(jnp.int32)
        if wanted:
            active = count
    return active


def block_rows(q_ref, k):
    return q_ref[pl.ds(pl.multiple_of(k * QT, QT), QT), :]


def fetch_all(pairs, sems):
    fetches = [pltpu.make_async_copy(src, dst, sems.at[i]) for i, (src, dst) in enumerate(pairs)]
    for fetch in fetches:
        fetch.start()
    return [fetch.wait for fetch in fetches]


def task_sim(p_ref, q_ref, k):
    return lax.dot_general(p_ref[...], block_rows(q_ref, k), turned_dims, preferred_element_type=f32)


def scores_kernel(mask_hbm, pos_hbm, q_hbm, p_hbm, send_ref, logit_ref, tot_ref, q_ref, turn_ref, *rest):
    blocks = tot_ref.shape[0]
    groups = blocks // GROUP
    scaled_refs, (mask_s, pos_ref, p_ref, order, top_ref, sim_ref, sems) = rest[:groups], rest[groups:]
    pairs = ((mask_hbm, mask_s), (pos_hbm, pos_ref), (p_hbm, p_ref), (q_hbm, q_ref))
    mask_wait, pos_wait, p_wait, q_wait = fetch_all(pairs, sems)
    top_ref[...] = jnp.zeros_like(top_ref)
    tot_ref[...] = jnp.ones_like(tot_ref)
    mask_wait()
    count = list_tasks(mask_s, order)
    pos_wait()
    p_wait()
    turn_ref[...] = p_ref[...].astype(f32).T.astype(bf16)
    q_wait()
    for group, scaled_ref in enumerate(scaled_refs):

        @pl.when(count > group * GROUP)
        def _(group=group, scaled_ref=scaled_ref):
            for i in range(GROUP):
                k = order[group * GROUP + i]
                scaled = jnp.exp(task_sim(p_ref, q_ref, k))
                scaled_ref[i] = scaled
                tot_ref[k] = jnp.sum(scaled.reshape(LP, B, QT), axis=0)

    lane_block = iota((B, blocks * B), 1) // B
    active = jnp.zeros((B, blocks * B), jnp.int32)
    for k in range(blocks):
        active = jnp.where(lane_block == k, mask_s[k], active)
    active = active > 0
    def finish():
        score = pack_means(top_ref[...] + jnp.log(tot_ref[...]))
        logit = jnp.where(active, score / contrast_temp, very_low)
        logit_ref[...] = logit
        positive = (pos_ref[...] == iota(logit.shape, 0) + lax.axis_index("pa") * B) & active
        local_top = jnp.max(logit, axis=0, keepdims=True)
        scaled = jnp.where(active, jnp.exp(logit - local_top), 0.0)
        local_total = jnp.sum(scaled, axis=0, keepdims=True)
        local_pos = jnp.sum(jnp.where(positive, logit, 0.0), axis=0, keepdims=True)
        row = iota(logit.shape, 0)
        send = jnp.where(row == 0, local_top, jnp.where(row == 1, local_total, local_pos))
        send_ref[...] = jnp.broadcast_to(jnp.where(row < 3, send, 0.0)[None], send_ref.shape)

    finish()

    safe = (jnp.min(tot_ref[...]) > safe_low) & (jnp.max(tot_ref[...]) < safe_high)

    @pl.when(jnp.logical_not(safe))
    def _():
        for group, scaled_ref in enumerate(scaled_refs):

            @pl.when(count > group * GROUP)
            def _(group=group, scaled_ref=scaled_ref):
                @pl.loop(0, GROUP)
                def _(i):
                    k = order[group * GROUP + i]
                    sim_ref[...] = task_sim(p_ref, q_ref, k)
                    sim = sim_ref[...].reshape(LP, B, QT)
                    top = jnp.max(sim, axis=0)
                    scaled = jnp.exp(sim - top[None])
                    top_ref[k] = top
                    tot_ref[k] = jnp.sum(scaled, axis=0)
                    scaled_ref[i] = scaled.reshape(PT, QT)

        finish()


def grads_kernel(
    mask_hbm, pos_ref, stat_ref, logit_ref, tot_ref, q_ref, turn_ref, *rest
):
    blocks = tot_ref.shape[0]
    groups = blocks // GROUP
    scaled_refs, rest = rest[:groups], rest[groups:]
    loss_ref, keep_ref, give_ref, own_ref, send1_ref, send2_ref, send3_ref, *rest = rest
    mask_s, order, weight_ref, gp_ref, dsim_ref, sem = rest
    fetch = pltpu.make_async_copy(mask_hbm, mask_s, sem)
    fetch.start()
    stat = stat_ref[...]
    top = jnp.max(stat, axis=0)[:1]
    row = iota(stat.shape, 1)
    sums = jnp.sum(stat * jnp.where(row == 1, jnp.exp(stat[:, :1] - top[None]), 1.0), axis=0)
    glob_top, glob_total, glob_pos = top, sums[1:2], sums[2:3]
    loss_ref[...] = glob_top + jnp.log(glob_total) - glob_pos
    logit = logit_ref[...]
    active = logit > very_low / 2
    positive = (pos_ref[...] == iota(logit.shape, 0) + lax.axis_index("pa") * B) & active
    prob = jnp.where(active, jnp.exp(logit - glob_top) / glob_total, 0.0)
    coef = (prob - positive.astype(f32)) / (contrast_temp * LQ)
    weight_ref[...] = unpack(coef) / tot_ref[...]
    gp_ref[...] = jnp.zeros_like(gp_ref)
    fetch.wait()
    count = list_tasks(mask_s, order)
    core = lax.rem(lax.axis_index("pa"), 2)
    for group, scaled_ref in enumerate(scaled_refs):

        @pl.when(count > group * GROUP)
        def _(group=group, scaled_ref=scaled_ref):
            tasks = [order[group * GROUP + i] for i in range(GROUP)]
            for i, k in enumerate(tasks):
                dsim = (scaled_ref[i].reshape(LP, B, QT) * weight_ref[k][None]).astype(bf16)
                dsim_ref[:, i * QT : (i + 1) * QT] = dsim.reshape(PT, QT)
            queries = jnp.concatenate([block_rows(q_ref, k) for k in tasks], axis=0)
            gp_ref[...] += jnp.dot(dsim_ref[...], queries, preferred_element_type=f32)
            turned = jnp.dot(turn_ref[...], dsim_ref[...], preferred_element_type=f32)
            for i, k in enumerate(tasks):
                first, second = (turned[:, i * QT + j * D : i * QT + (j + 1) * D] for j in range(2))
                keep_ref[k] = jnp.where(core == 0, first, second)
                give_ref[k] = jnp.where(core == 0, second, first)

        @pl.when(count <= group * GROUP)
        def _(group=group):
            for i in range(GROUP):
                keep_ref[order[group * GROUP + i]] = jnp.zeros(keep_ref.shape[1:], f32)
                give_ref[order[group * GROUP + i]] = jnp.zeros(give_ref.shape[1:], f32)

    mine = lax.axis_index("pb")
    piece = PT // 4

    def rows_of(owner):
        return gp_ref[pl.ds(pl.multiple_of(owner * piece, B), piece), :]

    own_ref[...] = rows_of(mine)
    for s, send in ((1, send1_ref), (2, send2_ref), (3, send3_ref)):
        send[...] = rows_of(lax.rem(mine + s, 4)).astype(bf16)


def sum_kernel(own_ref, a_ref, b_ref, c_ref, out_ref):
    total = own_ref[...] + a_ref[...].astype(f32) + b_ref[...].astype(f32) + c_ref[...].astype(f32)
    out_ref[...] = total.astype(bf16)


def both_kernel(keep_ref, got_ref, out_ref):
    out_ref[...] = (keep_ref[...] + got_ref[...]).astype(bf16)


def place_kernel(loss_ref, own_ref, a_ref, b_ref, c_ref, gp_ref, rows_ref):
    mine = lax.axis_index("pb")
    piece = PT // 4
    for s, ref in ((0, own_ref), (1, a_ref), (2, b_ref), (3, c_ref)):
        owner = lax.rem(mine + 4 - s, 4)
        gp_ref[pl.ds(pl.multiple_of(owner * piece, B), piece), :] = ref[...].astype(f32)
    count, own = loss_ref.shape[1], rows_ref.shape[1]
    pick = iota((count, own), 0) == iota((count, own), 1) + own * lax.axis_index("pa")
    rows_ref[...] = exact_dot(loss_ref[...], pick.astype(f32))


def rows_kernel(terms_ref, gq_ref):
    total = terms_ref[0].astype(f32)
    for i in range(1, terms_ref.shape[0]):
        total += terms_ref[i].astype(f32)
    gq_ref[...] = total.T


def in_hbm(x):
    return pltpu.with_memory_space_constraint(x, pltpu.HBM)


def call(kernel, out, specs, scratch=(), vmem=16 << 20, flops=0, nbytes=0):
    return pl.pallas_call(
        kernel,
        out_shape=out,
        in_specs=list(specs),
        out_specs=jax.tree.map(lambda _: VMEM, out),
        scratch_shapes=list(scratch),
        compiler_params=pltpu.CompilerParams(vmem_limit_bytes=vmem),
        cost_estimate=pl.CostEstimate(flops=flops, bytes_accessed=nbytes, transcendentals=0),
    )


def turn(x, s):
    return lax.ppermute(x, "pb", [(i, (i + s) % 4) for i in range(4)])


def on_device(queries, passages, pair_mask, positive):
    rows = queries.shape[0]
    blocks = rows // B
    groups = blocks // GROUP
    peers = lax.axis_size("pa")
    own_rows = rows // peers
    shape = jax.ShapeDtypeStruct
    flat_q = queries.reshape(rows * LQ, D)
    flat_p = jnp.swapaxes(passages, 0, 1).reshape(PT, D)
    mask = pair_mask.reshape(blocks)
    pos = positive.reshape(1, rows)
    ints = pltpu.SMEM((blocks,), jnp.int32)
    mask, flat_q, flat_p = (in_hbm(x) for x in (mask, flat_q, flat_p))
    wide = shape((blocks, B, QT), f32)
    packed = shape((B, rows), f32)
    send, logit, tot, near_q, turned_p, *scaled = call(
        scores_kernel,
        (
            shape((peers, B, rows), f32),
            packed,
            wide,
            shape((rows * LQ, D), bf16),
            shape((D, PT), bf16),
            *(shape((GROUP, PT, QT), f32),) * groups,
        ),
        (ANY,) * 4,
        [
            ints,
            pltpu.VMEM((1, rows), jnp.int32),
            pltpu.VMEM((PT, D), bf16),
            ints,
            pltpu.VMEM((blocks, B, QT), f32),
            pltpu.VMEM((PT, QT), f32),
            pltpu.SemaphoreType.DMA((4,)),
        ],
        flops=2_000_000_000,
        nbytes=3_000_000,
    )(mask, in_hbm(pos), flat_q, flat_p)
    stats = lax.all_to_all(send, "pa", 0, 0, tiled=True)
    piece = shape((PT // 4, D), bf16)
    half = shape((blocks, D, own_rows * LQ), f32)
    loss, keep, give, own, send1, send2, send3 = call(
        grads_kernel,
        (
            shape((1, rows), f32),
            half,
            half,
            shape((PT // 4, D), f32),
            piece,
            piece,
            piece,
        ),
        (ANY,) + (VMEM,) * (6 + groups),
        [
            ints,
            ints,
            pltpu.VMEM((blocks, B, QT), f32),
            pltpu.VMEM((PT, D), f32),
            pltpu.VMEM((PT, GROUP * QT), bf16),
            pltpu.SemaphoreType.DMA,
        ],
        flops=5_000_000_000,
        nbytes=5_000_000,
    )(mask, pos, stats, logit, tot, near_q, turned_p, *scaled)
    sends = {1: send1, 2: send2, 3: send3}
    got = [turn(sends[s], s) for s in (3, 2, 1)]
    got_half = lax.ppermute(give, "pa", [(i, i ^ 1) for i in range(peers)])
    both = call(both_kernel, shape(half.shape, bf16), (VMEM,) * 2, flops=10_000_000_000)(keep, got_half)
    same_core = [list(range(core, peers, 2)) for core in range(2)]
    gq_terms = lax.all_to_all(both, "pa", 0, 0, axis_index_groups=same_core, tiled=True)
    mine = call(sum_kernel, piece, (VMEM,) * 4, flops=30_000_000_000)(own, *got)
    others = [turn(mine, s) for s in (1, 2, 3)]
    flat, loss_rows = call(
        place_kernel, (shape((PT, D), f32), shape((1, own_rows), f32)), (VMEM,) * 5, nbytes=1_000_000
    )(loss, mine, *others)
    grad_q = call(rows_kernel, shape((own_rows * LQ, D), f32), (VMEM,), nbytes=1_000_000)(gq_terms)
    grad_p = jnp.swapaxes(flat.reshape(LP, B, D), 0, 1)
    return loss_rows.reshape(own_rows), grad_q.reshape(own_rows, LQ, D), grad_p


def solution(mesh):
    placed = (P("pb", None, None), P("pa", None, None), P("pb", "pa"), P("pb"))
    return jax.shard_map(
        on_device,
        mesh=mesh,
        in_specs=placed,
        out_specs=(P(("pb", "pa")), P(("pb", "pa"), None, None), P("pa", None, None)),
        check_vma=False,
    )
```

```python
import jax
import jax.numpy as jnp
from jax import lax
from jax.experimental import pallas as pl
from jax.experimental.pallas import tpu as pltpu
from jax.sharding import PartitionSpec as P

very_low = -1e30
contrast_temp = 0.05
safe_low, safe_high = 1e-12, 1e12
f32, bf16 = jnp.float32, jnp.bfloat16
VMEM = pl.BlockSpec(memory_space=pltpu.VMEM)
ANY = pl.BlockSpec(memory_space=pl.ANY)
B, LQ, LP, D = 8, 32, 180, 128
QT = B * LQ
PT = B * LP
GROUP = 4
turned_dims = (((1,), (1,)), ((), ()))


def iota(shape, dim):
    return lax.broadcasted_iota(jnp.int32, shape, dim)


def exact_dot(a, b):
    return jnp.dot(a, b, precision=lax.Precision.HIGHEST, preferred_element_type=f32)


def own_lanes(blocks):
    return iota((blocks, B, blocks * B), 2) // B == iota((blocks, B, blocks * B), 0)


def pack_means(wide):
    blocks = wide.shape[0]
    count = blocks * B
    pick = (iota((QT, count), 0) // LQ == iota((QT, count), 1) % B).astype(f32)
    sums = exact_dot(wide.reshape(count, QT), pick).reshape(blocks, B, count)
    return jnp.sum(jnp.where(own_lanes(blocks), sums, 0.0), axis=0) / LQ


def unpack(packed):
    count = packed.shape[1]
    blocks = count // B
    pick = (iota((count, QT), 0) % B == iota((count, QT), 1) // LQ).astype(f32)
    spread = jnp.where(own_lanes(blocks), packed[None], 0.0).reshape(count, count)
    return exact_dot(spread, pick).reshape(blocks, B, QT)


def list_tasks(mask_s, order):
    blocks = mask_s.shape[0]
    count = jnp.int32(0)
    for wanted in (True, False):
        for k in range(blocks):
            here = (mask_s[k] > 0) == wanted

            @pl.when(here)
            def _(k=k, count=count):
                order[count] = k

            count = count + here.astype(jnp.int32)
        if wanted:
            active = count
    return active


def block_rows(q_ref, k):
    return q_ref[pl.ds(pl.multiple_of(k * QT, QT), QT), :]


def fetch_all(pairs, sems):
    fetches = [pltpu.make_async_copy(src, dst, sems.at[i]) for i, (src, dst) in enumerate(pairs)]
    for fetch in fetches:
        fetch.start()
    return [fetch.wait for fetch in fetches]


def task_sim(p_ref, q_ref, k):
    return lax.dot_general(p_ref[...], block_rows(q_ref, k), turned_dims, preferred_element_type=f32)


def scores_kernel(mask_hbm, pos_hbm, q_hbm, p_hbm, send_ref, logit_ref, tot_ref, q_ref, turn_ref, *rest):
    blocks = tot_ref.shape[0]
    groups = blocks // GROUP
    scaled_refs, (mask_s, pos_ref, p_ref, order, top_ref, sim_ref, sems) = rest[:groups], rest[groups:]
    pairs = ((mask_hbm, mask_s), (pos_hbm, pos_ref), (p_hbm, p_ref), (q_hbm, q_ref))
    mask_wait, pos_wait, p_wait, q_wait = fetch_all(pairs, sems)
    top_ref[...] = jnp.zeros_like(top_ref)
    tot_ref[...] = jnp.ones_like(tot_ref)
    mask_wait()
    count = list_tasks(mask_s, order)
    pos_wait()
    p_wait()
    turn_ref[...] = p_ref[...].astype(f32).T.astype(bf16)
    q_wait()
    for group, scaled_ref in enumerate(scaled_refs):

        @pl.when(count > group * GROUP)
        def _(group=group, scaled_ref=scaled_ref):
            for i in range(GROUP):
                k = order[group * GROUP + i]
                scaled = jnp.exp(task_sim(p_ref, q_ref, k))
                scaled_ref[i] = scaled
                tot_ref[k] = jnp.sum(scaled.reshape(LP, B, QT), axis=0)

    lane_block = iota((B, blocks * B), 1) // B
    active = jnp.zeros((B, blocks * B), jnp.int32)
    for k in range(blocks):
        active = jnp.where(lane_block == k, mask_s[k], active)
    active = active > 0
    def finish():
        score = pack_means(top_ref[...] + jnp.log(tot_ref[...]))
        logit = jnp.where(active, score / contrast_temp, very_low)
        logit_ref[...] = logit
        positive = (pos_ref[...] == iota(logit.shape, 0) + lax.axis_index("pa") * B) & active
        local_top = jnp.max(logit, axis=0, keepdims=True)
        scaled = jnp.where(active, jnp.exp(logit - local_top), 0.0)
        local_total = jnp.sum(scaled, axis=0, keepdims=True)
        local_pos = jnp.sum(jnp.where(positive, logit, 0.0), axis=0, keepdims=True)
        row = iota(logit.shape, 0)
        send = jnp.where(row == 0, local_top, jnp.where(row == 1, local_total, local_pos))
        send_ref[...] = jnp.broadcast_to(jnp.where(row < 3, send, 0.0)[None], send_ref.shape)

    finish()

    safe = (jnp.min(tot_ref[...]) > safe_low) & (jnp.max(tot_ref[...]) < safe_high)

    @pl.when(jnp.logical_not(safe))
    def _():
        for group, scaled_ref in enumerate(scaled_refs):

            @pl.when(count > group * GROUP)
            def _(group=group, scaled_ref=scaled_ref):
                @pl.loop(0, GROUP)
                def _(i):
                    k = order[group * GROUP + i]
                    sim_ref[...] = task_sim(p_ref, q_ref, k)
                    sim = sim_ref[...].reshape(LP, B, QT)
                    top = jnp.max(sim, axis=0)
                    scaled = jnp.exp(sim - top[None])
                    top_ref[k] = top
                    tot_ref[k] = jnp.sum(scaled, axis=0)
                    scaled_ref[i] = scaled.reshape(PT, QT)

        finish()


def grads_kernel(
    mask_hbm, pos_ref, stat_ref, logit_ref, tot_ref, q_ref, turn_ref, *rest
):
    blocks = tot_ref.shape[0]
    groups = blocks // GROUP
    scaled_refs, rest = rest[:groups], rest[groups:]
    loss_ref, keep_ref, give_ref, own_ref, send1_ref, send2_ref, send3_ref, *rest = rest
    mask_s, order, weight_ref, gp_ref, dsim_ref, sem = rest
    fetch = pltpu.make_async_copy(mask_hbm, mask_s, sem)
    fetch.start()
    stat = stat_ref[...]
    top = jnp.max(stat, axis=0)[:1]
    row = iota(stat.shape, 1)
    sums = jnp.sum(stat * jnp.where(row == 1, jnp.exp(stat[:, :1] - top[None]), 1.0), axis=0)
    glob_top, glob_total, glob_pos = top, sums[1:2], sums[2:3]
    loss_ref[...] = glob_top + jnp.log(glob_total) - glob_pos
    logit = logit_ref[...]
    active = logit > very_low / 2
    positive = (pos_ref[...] == iota(logit.shape, 0) + lax.axis_index("pa") * B) & active
    prob = jnp.where(active, jnp.exp(logit - glob_top) / glob_total, 0.0)
    coef = (prob - positive.astype(f32)) / (contrast_temp * LQ)
    weight_ref[...] = unpack(coef) / tot_ref[...]
    fetch.wait()
    count = list_tasks(mask_s, order)

    @pl.when(count <= 0)
    def _():
        gp_ref[...] = jnp.zeros_like(gp_ref)

    core = lax.rem(lax.axis_index("pa"), 2)
    for group, scaled_ref in enumerate(scaled_refs):

        @pl.when(count > group * GROUP)
        def _(group=group, scaled_ref=scaled_ref):
            tasks = [order[group * GROUP + i] for i in range(GROUP)]
            for i, k in enumerate(tasks):
                dsim = (scaled_ref[i].reshape(LP, B, QT) * weight_ref[k][None]).astype(bf16)
                dsim_ref[:, i * QT : (i + 1) * QT] = dsim.reshape(PT, QT)
            queries = jnp.concatenate([block_rows(q_ref, k) for k in tasks], axis=0)
            terms = jnp.dot(dsim_ref[...], queries, preferred_element_type=f32)
            gp_ref[...] = terms if group == 0 else gp_ref[...] + terms
            turned = jnp.dot(turn_ref[...], dsim_ref[...], preferred_element_type=f32)
            for i, k in enumerate(tasks):
                first, second = (turned[:, i * QT + j * D : i * QT + (j + 1) * D] for j in range(2))
                keep_ref[k] = jnp.where(core == 0, first, second)
                give_ref[k] = jnp.where(core == 0, second, first)

        @pl.when(count <= group * GROUP)
        def _(group=group):
            for i in range(GROUP):
                keep_ref[order[group * GROUP + i]] = jnp.zeros(keep_ref.shape[1:], f32)
                give_ref[order[group * GROUP + i]] = jnp.zeros(give_ref.shape[1:], f32)

    mine = lax.axis_index("pb")
    piece = PT // 4

    def rows_of(owner):
        return gp_ref[pl.ds(pl.multiple_of(owner * piece, B), piece), :]

    own_ref[...] = rows_of(mine)
    for s, send in ((1, send1_ref), (2, send2_ref), (3, send3_ref)):
        send[...] = rows_of(lax.rem(mine + s, 4)).astype(bf16)


def sum_kernel(own_ref, a_ref, b_ref, c_ref, out_ref):
    total = own_ref[...] + a_ref[...].astype(f32) + b_ref[...].astype(f32) + c_ref[...].astype(f32)
    out_ref[...] = total.astype(bf16)


def both_kernel(keep_ref, got_ref, out_ref):
    out_ref[...] = (keep_ref[...] + got_ref[...]).astype(bf16)


def place_kernel(loss_ref, own_ref, a_ref, b_ref, c_ref, gp_ref, rows_ref):
    mine = lax.axis_index("pb")
    piece = PT // 4
    for s, ref in ((0, own_ref), (1, a_ref), (2, b_ref), (3, c_ref)):
        owner = lax.rem(mine + 4 - s, 4)
        gp_ref[pl.ds(pl.multiple_of(owner * piece, B), piece), :] = ref[...].astype(f32)
    count, own = loss_ref.shape[1], rows_ref.shape[1]
    pick = iota((count, own), 0) == iota((count, own), 1) + own * lax.axis_index("pa")
    rows_ref[...] = exact_dot(loss_ref[...], pick.astype(f32))


def rows_kernel(terms_ref, gq_ref):
    total = terms_ref[0].astype(f32)
    for i in range(1, terms_ref.shape[0]):
        total += terms_ref[i].astype(f32)
    gq_ref[...] = total.T


def in_hbm(x):
    return pltpu.with_memory_space_constraint(x, pltpu.HBM)


def call(kernel, out, specs, scratch=(), vmem=16 << 20, flops=0, nbytes=0):
    return pl.pallas_call(
        kernel,
        out_shape=out,
        in_specs=list(specs),
        out_specs=jax.tree.map(lambda _: VMEM, out),
        scratch_shapes=list(scratch),
        compiler_params=pltpu.CompilerParams(vmem_limit_bytes=vmem),
        cost_estimate=pl.CostEstimate(flops=flops, bytes_accessed=nbytes, transcendentals=0),
    )


def turn(x, s):
    return lax.ppermute(x, "pb", [(i, (i + s) % 4) for i in range(4)])


def on_device(queries, passages, pair_mask, positive):
    rows = queries.shape[0]
    blocks = rows // B
    groups = blocks // GROUP
    peers = lax.axis_size("pa")
    own_rows = rows // peers
    shape = jax.ShapeDtypeStruct
    flat_q = queries.reshape(rows * LQ, D)
    flat_p = jnp.swapaxes(passages, 0, 1).reshape(PT, D)
    mask = pair_mask.reshape(blocks)
    pos = positive.reshape(1, rows)
    ints = pltpu.SMEM((blocks,), jnp.int32)
    mask, flat_q, flat_p = (in_hbm(x) for x in (mask, flat_q, flat_p))
    wide = shape((blocks, B, QT), f32)
    packed = shape((B, rows), f32)
    send, logit, tot, near_q, turned_p, *scaled = call(
        scores_kernel,
        (
            shape((peers, B, rows), f32),
            packed,
            wide,
            shape((rows * LQ, D), bf16),
            shape((D, PT), bf16),
            *(shape((GROUP, PT, QT), f32),) * groups,
        ),
        (ANY,) * 4,
        [
            ints,
            pltpu.VMEM((1, rows), jnp.int32),
            pltpu.VMEM((PT, D), bf16),
            ints,
            pltpu.VMEM((blocks, B, QT), f32),
            pltpu.VMEM((PT, QT), f32),
            pltpu.SemaphoreType.DMA((4,)),
        ],
        flops=2_000_000_000,
        nbytes=3_000_000,
    )(mask, in_hbm(pos), flat_q, flat_p)
    stats = lax.all_to_all(send, "pa", 0, 0, tiled=True)
    piece = shape((PT // 4, D), bf16)
    half = shape((blocks, D, own_rows * LQ), f32)
    loss, keep, give, own, send1, send2, send3 = call(
        grads_kernel,
        (
            shape((1, rows), f32),
            half,
            half,
            shape((PT // 4, D), f32),
            piece,
            piece,
            piece,
        ),
        (ANY,) + (VMEM,) * (6 + groups),
        [
            ints,
            ints,
            pltpu.VMEM((blocks, B, QT), f32),
            pltpu.VMEM((PT, D), f32),
            pltpu.VMEM((PT, GROUP * QT), bf16),
            pltpu.SemaphoreType.DMA,
        ],
        flops=5_000_000_000,
        nbytes=5_000_000,
    )(mask, pos, stats, logit, tot, near_q, turned_p, *scaled)
    sends = {1: send1, 2: send2, 3: send3}
    got = [turn(sends[s], s) for s in (3, 2, 1)]
    got_half = lax.ppermute(give, "pa", [(i, i ^ 1) for i in range(peers)])
    both = call(both_kernel, shape(half.shape, bf16), (VMEM,) * 2, flops=10_000_000_000)(keep, got_half)
    same_core = [list(range(core, peers, 2)) for core in range(2)]
    gq_terms = lax.all_to_all(both, "pa", 0, 0, axis_index_groups=same_core, tiled=True)
    mine = call(sum_kernel, piece, (VMEM,) * 4, flops=30_000_000_000)(own, *got)
    others = [turn(mine, s) for s in (1, 2, 3)]
    flat, loss_rows = call(
        place_kernel, (shape((PT, D), f32), shape((1, own_rows), f32)), (VMEM,) * 5, nbytes=1_000_000
    )(loss, mine, *others)
    grad_q = call(rows_kernel, shape((own_rows * LQ, D), f32), (VMEM,), nbytes=1_000_000)(gq_terms)
    grad_p = jnp.swapaxes(flat.reshape(LP, B, D), 0, 1)
    return loss_rows.reshape(own_rows), grad_q.reshape(own_rows, LQ, D), grad_p


def solution(mesh):
    placed = (P("pb", None, None), P("pa", None, None), P("pb", "pa"), P("pb"))
    return jax.shard_map(
        on_device,
        mesh=mesh,
        in_specs=placed,
        out_specs=(P(("pb", "pa")), P(("pb", "pa"), None, None), P("pa", None, None)),
        check_vma=False,
    )
```
